256 devices in a mesh: tm: 8 (over z), space: 32 (over y, x, core).
Axes of the slice: x: 4, y: 4, z: 8, core: 2. Of those that a mesh axis runs over, the one named last changes fastest.
Arguments:
- features: bfloat16 [32, 256, 128, 128], P('tm', 'space'), may hold values from -45 to 45
- gain_one: float32 [128], replicated, may hold values from 0.1 to 1.9
- shift_one: float32 [128], replicated, may hold values from -3 to 3
- kernel_one: bfloat16 [3, 3, 3, 128, 128], replicated, may hold values from -0.109375 to 0.109375
- bias_one: float32 [128], replicated, may hold values from -3 to 3
- gain_two: float32 [128], replicated, may hold values from 0.1 to 1.9
- shift_two: float32 [128], replicated, may hold values from -3 to 3
- kernel_two: bfloat16 [3, 3, 3, 128, 128], replicated, may hold values from -0.109375 to 0.109375
- bias_two: float32 [128], replicated, may hold values from -3 to 3
Outputs:
- decoded: float32 [32, 256, 128, 128], P('tm', 'space')
The draws below stay inside these ranges and needn't reach their ends.
All inputs are finite; a program needn't handle non-finite values.
Results may differ from the reference program's by a relative error of at most 0.0014.
Values may be sent and summed in bfloat16 or wider, within the bound.
No kernel may reach another device: no remote copies, remote signals or barrier semaphores. Data moves between devices by JAX's collectives and lax.ppermute only.
A program may use at most 128 MiB of HBM per device.

```python
import math
import jax
import jax.numpy as jnp
from jax import lax

C = 128
GROUPS = 32
W = 128
NT = 32
NH = 256


def draw_features(key, part):
    key = jax.random.fold_in(key, 11)
    key_chan, key_base = jax.random.split(key, 2)
    channel_scale = 0.3 * jnp.exp(jax.random.uniform(key_chan, (C,), jnp.float32, 0.0, math.log(10.0)))
    time_pos = jnp.arange(NT, dtype=jnp.float32) / max(NT - 1, 1)
    row_pos = jnp.arange(NH, dtype=jnp.float32) / max(NH - 1, 1)
    trend = jnp.power(3.0, time_pos - 0.5)[:, None, None, None] * jnp.power(3.0, row_pos - 0.5)[None, :, None, None]
    shape = (NT, NH, W, C)
    values = jnp.clip(jax.random.normal(key_base, shape, jnp.float32), -5.0, 5.0)
    values = values * channel_scale * trend
    return jnp.clip(values, -45.0, 45.0).astype(jnp.bfloat16)


def noise(rng, shape, scale, most, held_as=jnp.bfloat16):
    array = scale * jax.random.normal(rng, shape, jnp.float32)
    return jnp.clip(array, min=-most, max=most).astype(held_as)


def setup_inputs(seed: int = 0) -> dict:
    streams_of = jax.random.split(jax.random.key(seed), 10)
    features = draw_features(jax.random.fold_in(streams_of[9], 71), 0)
    gain_one = jnp.clip(1.0 + 0.18 * jax.random.normal(streams_of[1], (C,), jnp.float32), 0.1, 1.9)
    shift_one = noise(streams_of[2], (C,), 0.5, 3.0, jnp.float32)
    kernel_one = noise(streams_of[3], (3, 3, 3, C, C), (27 * C) ** -0.5, 0.109375)
    bias_one = noise(streams_of[4], (C,), 0.5, 3.0, jnp.float32)
    gain_two = jnp.clip(1.0 + 0.18 * jax.random.normal(streams_of[5], (C,), jnp.float32), 0.1, 1.9)
    shift_two = noise(streams_of[6], (C,), 0.5, 3.0, jnp.float32)
    kernel_two = noise(streams_of[7], (3, 3, 3, C, C), (27 * C) ** -0.5, 0.109375)
    bias_two = noise(streams_of[8], (C,), 0.5, 3.0, jnp.float32)
    return dict(features=features, gain_one=gain_one, shift_one=shift_one, kernel_one=kernel_one, bias_one=bias_one, gain_two=gain_two, shift_two=shift_two, kernel_two=kernel_two, bias_two=bias_two)


EPS = 1e-06

def act_norm(field, gain, shift):
    values = field.astype(jnp.float32)
    width = values.shape[-1]
    grouped = values.reshape(values.shape[:-1] + (GROUPS, width // GROUPS))
    mean = lax.optimization_barrier(jnp.mean(grouped, axis=(0, 1, 2, 4)))
    deviation = grouped - mean[:, None]
    var = lax.optimization_barrier(jnp.mean(deviation * deviation, axis=(0, 1, 2, 4)))
    normed = (deviation * lax.rsqrt(var + EPS)[:, None]).reshape(values.shape)
    return jax.nn.silu(normed * gain + shift).astype(jnp.bfloat16)

def causal_conv(field, kernel, bias):
    frames, rows, cols, width = field.shape
    padded = jnp.concatenate([field[:1], field[:1], field], axis=0)
    padded = jnp.pad(padded, ((0, 0), (1, 1), (1, 1), (0, 0)))
    flat_kernel = kernel.reshape(27 * width, width).astype(jnp.float32)

    def one_frame(index):
        window = lax.dynamic_slice_in_dim(padded, index, 3, 0)
        pieces = []
        for step_t in range(3):
            for step_r in range(3):
                for step_c in range(3):
                    pieces.append(window[step_t, step_r:step_r + rows, step_c:step_c + cols, :])
        patches = jnp.concatenate(pieces, axis=-1).astype(jnp.float32).reshape(rows * cols, 27 * width)
        result = jnp.dot(patches, flat_kernel, preferred_element_type=jnp.float32)
        return result.reshape(rows, cols, width) + bias
    return lax.map(one_frame, jnp.arange(frames, dtype=jnp.int32))

def reference(features, gain_one, shift_one, kernel_one, bias_one, gain_two, shift_two, kernel_two, bias_two):
    first = act_norm(features, gain_one, shift_one)
    inner = causal_conv(first, kernel_one, bias_one)
    second = act_norm(inner, gain_two, shift_two)
    outer = causal_conv(second, kernel_two, bias_two)
    return features.astype(jnp.float32) + outer
```

```python
import functools

import jax
import jax.numpy as jnp
from jax import lax
from jax.experimental import pallas as pl
from jax.experimental.pallas import tpu as pltpu
from jax.sharding import PartitionSpec as P

EPS = 1e-06
MEMBERS = 4
BOTH = ("tm", "space")
F32 = jnp.float32
BF16 = jnp.bfloat16


def lane_of(shape):
    return lax.broadcasted_iota(jnp.int32, shape, len(shape) - 1)


def group_sum(v):
    lane = lane_of(v.shape)
    width = v.shape[-1]
    axis = v.ndim - 1
    v = v + jnp.where((lane & 1) == 1, pltpu.roll(v, 1, axis), pltpu.roll(v, width - 1, axis))
    return v + jnp.where((lane & 2) == 2, pltpu.roll(v, 2, axis), pltpu.roll(v, width - 2, axis))


def column_sum(v):
    return jnp.broadcast_to(jnp.sum(v, axis=0, keepdims=True), (8, v.shape[1]))


def local_stats(load, rows, cells):
    def add(i, total):
        return total + load(i)

    zero = jnp.zeros((128, 128), F32)
    mean = group_sum(column_sum(lax.fori_loop(0, rows, add, zero, unroll=4))) / cells

    def spread(i, total):
        d = load(i) - mean[:1]
        return total + d * d

    return mean, group_sum(column_sum(lax.fori_loop(0, rows, spread, zero, unroll=4)))


def payload(mean, spread, extra):
    place = lane_of(mean.shape) & 3
    return jnp.where(place == 0, mean, jnp.where(place == 1, spread, jnp.where(place == 2, extra, 0.0)))


def pick(rows, place):
    return group_sum(jnp.where((lane_of(rows.shape) & 3) == place, rows, 0.0))


def whole_stats(got_ref, cells):
    got = got_ref[...]
    devices = got.shape[0]
    place = lane_of(got.shape) & 3
    means = jnp.where(place == 0, got, 0.0)
    mean = group_sum(column_sum(means)) / devices
    spread = group_sum(column_sum(jnp.where(place == 1, got, 0.0)))
    off = jnp.where(place == 0, got - mean[:1], 0.0)
    between = group_sum(column_sum(off * off))
    var = (spread + between * cells) / (cells * devices)
    return mean, lax.rsqrt(var + EPS)


def put_act(x, mean, slope, half_shift, keep, out, f, r):
    h = (x - mean) * slope + half_shift
    y = h + h * jnp.tanh(h)
    if keep is not None:
        y = y * keep
    row = lax.broadcasted_iota(jnp.int32, y.shape, 0)
    out[0, f, r] = jnp.where(row == 0, 0.0, pltpu.roll(y, 1, 0)).astype(BF16)
    out[1, f, r] = y.astype(BF16)
    out[2, f, r] = jnp.where(row == 127, 0.0, pltpu.roll(y, 127, 0)).astype(BF16)


def build_taps(kernel_ref, taps):
    zero = jnp.zeros((9 * 128, 128), BF16)
    for f in range(4):
        at = pl.ds(f * 9 * 128, 9 * 128)
        taps[at, :128] = kernel_ref[f] if f < 3 else zero
        taps[at, 128:] = kernel_ref[f - 1] if f > 0 else zero


def conv_rows(acts, taps, r, count):
    pieces = []
    for f in range(4):
        for i in range(3):
            for j in range(3):
                pieces.append(acts[j, f, pl.ds(r + i, count)].reshape(count * 128, 128))
    return jnp.dot(jnp.concatenate(pieces, axis=-1), taps[...], preferred_element_type=F32)


def stats_kernel(x_ref, out_ref):
    rows = x_ref.shape[0] * x_ref.shape[1]
    per = x_ref.shape[1]
    load = lambda i: x_ref[i // per, i % per].astype(F32)
    mean, spread = local_stats(load, rows, float(rows * 128 * MEMBERS))
    out_ref[...] = jnp.broadcast_to(payload(mean, spread, mean)[:1], out_ref.shape)


def norm_constants(got_ref, gain_ref, shift_ref, cells):
    mean, scale = whole_stats(got_ref, cells)
    return mean[:1], scale[:1] * gain_ref[...] * 0.5, shift_ref[...] * 0.5


def first_kernel(early, cells, rc, place_ref, got_ref, gain_ref, shift_ref, kernel_ref, bias_ref, *refs):
    if early:
        x_ref, up_ref, down_ref, z_ref, zup_ref, zdown_ref, prev_ref, inner_ref, pay_ref, acts, taps = refs
    else:
        x_ref, up_ref, down_ref, inner_ref, part_ref, send_ref, acts, taps = refs
    mean, slope, half = norm_constants(got_ref, gain_ref, shift_ref, cells)
    build_taps(kernel_ref, taps)
    top = jnp.where(place_ref[1] == 0, 0.0, 1.0)
    bottom = jnp.where(place_ref[2] == 0, 0.0, 1.0)

    def frame(src, up, down, f_src, f):
        for r in range(2):
            put_act(up[f_src, r].astype(F32), mean, slope, half, top, acts, f, r)
            put_act(down[f_src, r].astype(F32), mean, slope, half, bottom, acts, f, 10 + r)

        def own(r, c):
            put_act(src[f_src, r].astype(F32), mean, slope, half, None, acts, f, 2 + r)
            return c

        lax.fori_loop(0, 8, own, 0, unroll=4)

    if early:
        for f in range(2):
            frame(x_ref, up_ref, down_ref, f, 2 + f)

        @pl.when(place_ref[0] == 0)
        def _():
            for f in range(2):
                for j in range(3):
                    acts[j, f] = acts[j, 2]

        @pl.when(place_ref[0] != 0)
        def _():
            for f in range(2):
                frame(z_ref, zup_ref, zdown_ref, f, f)
    else:
        for f in range(4):
            frame(x_ref, up_ref, down_ref, f, f)

    def rows(i, c):
        r = i * rc
        got = conv_rows(acts, taps, r, rc)
        for o in range(2):
            inner_ref[o, pl.ds(r, rc)] = (got[:, o * 128 : (o + 1) * 128] + bias_ref[...]).reshape(rc, 128, 128)
        return c

    lax.fori_loop(0, 10 // rc, rows, 0)
    half_cells = cells / 2
    load = lambda i: inner_ref[i // 8, 1 + i % 8]
    m, s = local_stats(load, 16, half_cells)
    if early:
        m_late, s_late = prev_ref[0], prev_ref[1]
        both = (m + m_late) * 0.5
        gap = m - m_late
        pay = payload(both, s + s_late + gap * gap * (half_cells / 2), m_late)
        pay_ref[...] = jnp.broadcast_to(pay[:1], pay_ref.shape)
    else:
        part_ref[0] = m
        part_ref[1] = s
        for o in range(2):
            send_ref[o] = (inner_ref[o] - m[:1]).astype(BF16)


def second_kernel(early, cells, rc, place_ref, got_ref, gain_ref, shift_ref, kernel_ref, bias_ref, *refs):
    if early:
        b_ref, z_ref, feat_ref, _, out_ref, acts, taps = refs
    else:
        b_ref, a_ref, feat_ref, out_ref, acts, taps = refs
    mean, slope, half = norm_constants(got_ref, gain_ref, shift_ref, cells)
    build_taps(kernel_ref, taps)
    top = jnp.where(place_ref[1] == 0, 0.0, 1.0)
    bottom = jnp.where(place_ref[2] == 0, 0.0, 1.0)

    def frame(src, f_src, f, base):
        put_act(src[f_src, 0].astype(F32), base, slope, half, top, acts, f, 0)
        put_act(src[f_src, 9].astype(F32), base, slope, half, bottom, acts, f, 9)

        def own(r, c):
            put_act(src[f_src, r].astype(F32), base, slope, half, None, acts, f, r)
            return c

        lax.fori_loop(1, 9, own, 0, unroll=4)

    if early:
        for f in range(2):
            frame(b_ref, f, 2 + f, mean)

        @pl.when(place_ref[0] == 0)
        def _():
            for f in range(2):
                for j in range(3):
                    acts[j, f] = acts[j, 2]

        @pl.when(place_ref[0] != 0)
        def _():
            sender = got_ref[pl.ds(place_ref[3], 1)]
            base = mean - pick(jnp.broadcast_to(sender, (8, 128)), 2)[:1]
            for f in range(2):
                frame(z_ref, f, f, base)
    else:
        for f in range(2):
            frame(b_ref, f, f, mean)
            frame(a_ref, f, 2 + f, mean)

    def rows(i, c):
        r = i * rc
        got = conv_rows(acts, taps, r, rc)
        for o in range(2):
            add = feat_ref[o, pl.ds(r, rc)].astype(F32)
            out_ref[o, pl.ds(r, rc)] = add + (got[:, o * 128 : (o + 1) * 128] + bias_ref[...]).reshape(rc, 128, 128)
        return c

    lax.fori_loop(0, 8 // rc, rows, 0)


VMEM = pl.BlockSpec(memory_space=pltpu.VMEM)
SMEM = pl.BlockSpec(memory_space=pltpu.SMEM)
PARAMS = pltpu.CompilerParams(vmem_limit_bytes=48 * 1024 * 1024)


def scratch(rows):
    return [pltpu.VMEM((3, 4, rows, 128, 128), BF16), pltpu.VMEM((36 * 128, 256), BF16)]


def cost(rows):
    return pl.CostEstimate(flops=2 * 2 * rows * 128 * 36 * 128 * 128, bytes_accessed=4 << 20, transcendentals=4 * rows * 128 * 128)


def shape(dims, dtype):
    return jax.ShapeDtypeStruct(dims, dtype)


def shards(features, gain_one, shift_one, kernel_one, bias_one, gain_two, shift_two, kernel_two, bias_two):
    slabs = lax.axis_size("tm")
    strips = lax.axis_size("space")
    tm = lax.axis_index("tm")
    space = lax.axis_index("space")
    devices = slabs * strips
    cells = float(4 * 8 * 128 * MEMBERS)
    before = jnp.maximum(tm - 1, 0) * strips + space
    place = jnp.stack([tm, space, strips - 1 - space, before]).astype(jnp.int32)
    down_pairs = [(i, i + 1) for i in range(strips - 1)]
    up_pairs = [(i + 1, i) for i in range(strips - 1)]
    later = [(i, i + 1) for i in range(slabs - 1)]
    row = lambda v: v.reshape(1, 128)
    taps_one = kernel_one.reshape(3, 9 * 128, 128)
    taps_two = kernel_two.reshape(3, 9 * 128, 128)

    z_one = lax.ppermute(features[2:], "tm", later)
    up = lax.ppermute(features[:, 6:], "space", down_pairs)
    down = lax.ppermute(features[:, :2], "space", up_pairs)
    pay = pl.pallas_call(
        stats_kernel, out_shape=shape((devices, 128), F32), in_specs=[VMEM], out_specs=VMEM,
        cost_estimate=pl.CostEstimate(flops=1 << 22, bytes_accessed=1 << 20, transcendentals=0), name="stats",
    )(features)
    got = lax.all_to_all(pay, BOTH, 0, 0)
    z_up = lax.ppermute(z_one[:, 6:], "space", down_pairs)
    z_down = lax.ppermute(z_one[:, :2], "space", up_pairs)
    head = (place, got, row(gain_one), row(shift_one), taps_one, row(bias_one))
    inner_a, part, send = pl.pallas_call(
        functools.partial(first_kernel, False, cells, 2),
        out_shape=[shape((2, 10, 128, 128), F32), shape((2, 8, 128), F32), shape((2, 10, 128, 128), BF16)],
        in_specs=[SMEM] + [VMEM] * 8, out_specs=[VMEM] * 3, scratch_shapes=scratch(12),
        compiler_params=PARAMS, cost_estimate=cost(10), name="first_late",
    )(*head, features, up, down)
    z_two = lax.ppermute(send, "tm", later)
    inner_b, pay = pl.pallas_call(
        functools.partial(first_kernel, True, cells, 2),
        out_shape=[shape((2, 10, 128, 128), F32), shape((devices, 128), F32)],
        in_specs=[SMEM] + [VMEM] * 12, out_specs=[VMEM] * 2, scratch_shapes=scratch(12),
        compiler_params=PARAMS, cost_estimate=cost(10), name="first_early",
    )(*head, features, up, down, z_one, z_up, z_down, part)
    got = lax.all_to_all(pay, BOTH, 0, 0)
    head = (place, got, row(gain_two), row(shift_two), taps_two, row(bias_two))
    block = lambda k: pl.BlockSpec((2, 8, 128, 128), lambda *_: (k, 0, 0, 0))
    out = pl.pallas_call(
        functools.partial(second_kernel, False, cells, 2), grid=(1,),
        out_shape=shape((4, 8, 128, 128), F32),
        in_specs=[SMEM] + [VMEM] * 7 + [block(1)], out_specs=block(1), scratch_shapes=scratch(10),
        compiler_params=PARAMS, cost_estimate=cost(8), name="second_late",
    )(*head, inner_b, inner_a, features)
    return pl.pallas_call(
        functools.partial(second_kernel, True, cells, 2), grid=(1,),
        out_shape=shape((4, 8, 128, 128), F32),
        in_specs=[SMEM] + [VMEM] * 7 + [block(0), pl.BlockSpec(memory_space=pl.ANY)], out_specs=block(0),
        scratch_shapes=scratch(10), input_output_aliases={9: 0},
        compiler_params=PARAMS, cost_estimate=cost(8), name="second_early",
    )(*head, inner_b, z_two, features, out)


def solution(mesh):
    placed = (P("tm", "space", None, None), P(), P(), P(), P(), P(), P(), P(), P())
    return jax.shard_map(
        shards, mesh=mesh, in_specs=placed, out_specs=P("tm", "space", None, None), check_vma=False
    )
```

```python
import functools

import jax
import jax.numpy as jnp
from jax import lax
from jax.experimental import pallas as pl
from jax.experimental.pallas import tpu as pltpu
from jax.sharding import PartitionSpec as P

EPS = 1e-06
MEMBERS = 4
LATE = 1
BOTH = ("tm", "space")
F32 = jnp.float32
BF16 = jnp.bfloat16


def lane_of(shape):
    return lax.broadcasted_iota(jnp.int32, shape, len(shape) - 1)


def group_sum(v):
    lane = lane_of(v.shape)
    width = v.shape[-1]
    axis = v.ndim - 1
    v = v + jnp.where((lane & 1) == 1, pltpu.roll(v, 1, axis), pltpu.roll(v, width - 1, axis))
    return v + jnp.where((lane & 2) == 2, pltpu.roll(v, 2, axis), pltpu.roll(v, width - 2, axis))


def column_sum(v):
    return jnp.broadcast_to(jnp.sum(v, axis=0, keepdims=True), (8, v.shape[1]))


def local_stats(load, rows, cells):
    total = load(0)
    for i in range(1, rows):
        total = total + load(i)
    mean = group_sum(column_sum(total)) / cells
    spread = jnp.zeros((128, 128), F32)
    for i in range(rows):
        d = load(i) - mean[:1]
        spread = spread + d * d
    return mean, group_sum(column_sum(spread))


def payload(mean, spread):
    place = lane_of(mean.shape) & 3
    return jnp.where(place == 0, mean, jnp.where(place == 1, spread, 0.0))


def pick(rows, place):
    return group_sum(jnp.where((lane_of(rows.shape) & 3) == place, rows, 0.0))


def whole_stats(got_ref, cells):
    got = got_ref[...]
    devices = got.shape[0]
    place = lane_of(got.shape) & 3
    means = jnp.where(place == 0, got, 0.0)
    mean = group_sum(column_sum(means)) / devices
    spread = group_sum(column_sum(jnp.where(place == 1, got, 0.0)))
    off = jnp.where(place == 0, got - mean[:1], 0.0)
    between = group_sum(column_sum(off * off))
    var = (spread + between * cells) / (cells * devices)
    return mean, lax.rsqrt(var + EPS)


def put_act(off, slope, half_shift, keep, out, f, r):
    h = off * slope + half_shift
    y = h + h * jnp.tanh(h)
    if keep is not None:
        y = y * keep
    row = lax.broadcasted_iota(jnp.int32, y.shape, 0)
    out[0, f, r] = jnp.where(row == 0, 0.0, pltpu.roll(y, 1, 0)).astype(BF16)
    out[1, f, r] = y.astype(BF16)
    out[2, f, r] = jnp.where(row == 127, 0.0, pltpu.roll(y, 127, 0)).astype(BF16)


def build_taps(kernel, taps):
    zero = jnp.zeros((9 * 128, 128), BF16)
    for f in range(4):
        at = pl.ds(f * 9 * 128, 9 * 128)
        taps[at, :128] = kernel[f] if f < 3 else zero
        taps[at, 128:] = kernel[f - 1] if f > 0 else zero


def conv_pair(acts, taps, first, rows):
    pieces = []
    for f in range(4):
        for i in range(3):
            for j in range(3):
                pieces.append(acts[j, first + f, pl.ds(i, rows)].reshape(rows * 128, 128))
    return jnp.dot(jnp.concatenate(pieces, axis=-1), taps[...], preferred_element_type=F32)


def stats_kernel(x_hbm, *refs):
    small, (x_ref, pay_ref, z_ref, in_ref, far_ref, small_ref, held, sems) = refs[:6], refs[6:]
    frames, per = x_ref.shape[:2]
    copies = [pltpu.make_async_copy(x_hbm.at[f], x_ref.at[f], sems.at[f]) for f in range(frames)]
    copies += [pltpu.make_async_copy(v, held.at[i], sems.at[frames + i]) for i, v in enumerate(small)]
    for copy in copies:
        copy.start()
    for copy in copies:
        copy.wait()
    small_ref[...] = held[...]
    z_ref[...] = x_ref[2:]
    odd = (lax.axis_index("space") & 1) == 1
    for f in range(4):
        for r in range(2):
            low, high = x_ref[f, r], x_ref[f, per - 2 + r]
            in_ref[f, r] = jnp.where(odd, low, high)
            far_ref[f, r] = jnp.where(odd, high, low)
    rows = frames * per
    load = lambda i: x_ref[i // per, i % per].astype(F32)
    mean, spread = local_stats(load, rows, float(rows * 128 * MEMBERS))
    pay_ref[...] = jnp.broadcast_to(payload(mean, spread)[:1], pay_ref.shape)


def norm_constants(got_ref, small_ref, at, cells):
    mean, scale = whole_stats(got_ref, cells)
    gain, shift, bias = (small_ref[at + i : at + i + 1] for i in range(3))
    return mean[:1], scale[:1] * gain * 0.5, shift * 0.5, bias


def edges(strips):
    space = lax.axis_index("space")
    return jnp.where(space == 0, 0.0, 1.0), jnp.where(space == strips - 1, 0.0, 1.0)


def first_kernel(cells, strips, kernel_hbm, got_ref, small_ref, x_ref, in_ref, far_ref,
                 z_ref, z_in_ref, z_far_ref, inner_ref, pay_ref, send_ref, acts, taps, kernel, sem):
    fetch = pltpu.make_async_copy(kernel_hbm, kernel, sem)
    fetch.start()
    mean, slope, half, bias = norm_constants(got_ref, small_ref, 0, cells)
    top, bottom = edges(strips)
    odd = (lax.axis_index("space") & 1) == 1
    start = lax.axis_index("tm") == 0

    def frame(own, near, far, f):
        for r in range(12):
            if 2 <= r < 10:
                x, keep = own(r - 2), None
            else:
                high = r >= 10
                i = r - 10 if high else r
                a, b = near(i), far(i)
                x, keep = (jnp.where(odd, b, a), bottom) if high else (jnp.where(odd, a, b), top)
            put_act(x.astype(F32) - mean, slope, half, keep, acts, f, r)

    def of(ref, f):
        return lambda r: ref[f, r]

    def carried(ref, z, f):
        return lambda r: jnp.where(start, ref[0, r], z[f, r])

    def conv(pair):
        got = conv_pair(acts, taps, 2 * pair, 10)
        for o in range(2):
            inner_ref[2 * pair + o] = (got[:, o * 128 : (o + 1) * 128] + bias).reshape(10, 128, 128)

    for f in range(4):
        if f == 2:
            fetch.wait()
            build_taps(kernel, taps)
        frame(of(x_ref, f), of(in_ref, f), of(far_ref, f), 2 + f)
    conv(1)
    for f in range(2):
        frame(carried(x_ref, z_ref, f), carried(in_ref, z_in_ref, f), carried(far_ref, z_far_ref, f), f)
    conv(0)
    load = lambda i: inner_ref[i // 8, 1 + i % 8]
    m, s = local_stats(load, 32, cells)
    pay_ref[...] = jnp.broadcast_to(payload(m, s)[:1], pay_ref.shape)
    for o in range(2):
        send_ref[o] = (inner_ref[2 + o] - m[:1]).astype(BF16)


def second_kernel(early, cells, strips, kernel_hbm, got_ref, small_ref, feat_ref, x_ref, *refs):
    if early:
        z_ref, _, out_hbm, acts, taps, kernel, out, sem, sems = refs
    else:
        out_hbm, acts, taps, kernel, out, sem, sems = refs
    base_frame = 0 if early else 2
    fetch = pltpu.make_async_copy(kernel_hbm, kernel, sem)
    fetch.start()
    mean, slope, half, bias = norm_constants(got_ref, small_ref, 3, cells)
    top, bottom = edges(strips)

    def frame(off, f):
        for r in range(10):
            put_act(off(r), slope, half, {0: top, 9: bottom}.get(r), acts, f, r)

    if early:
        tm = lax.axis_index("tm")
        start = tm == 0
        sender = got_ref[pl.ds(jnp.maximum(tm - 1, 0) * strips + lax.axis_index("space"), 1)]
        base = mean - pick(jnp.broadcast_to(sender, (8, 128)), 0)[:1]
    for f in range(4):
        if f == 2:
            fetch.wait()
            build_taps(kernel, taps)
        if not early:
            frame(lambda r: x_ref[f, r] - mean, f)
        elif f >= 2:
            frame(lambda r: x_ref[f - 2, r] - mean, f)
        else:
            frame(lambda r: jnp.where(start, x_ref[0, r] - mean, z_ref[f, r].astype(F32) - base), f)
    got = conv_pair(acts, taps, 0, 8)
    copies = []
    for o in range(2):
        conv = (got[:, o * 128 : (o + 1) * 128] + bias).reshape(8, 128, 128)
        out[o] = feat_ref[base_frame + o].astype(F32) + conv
        copies.append(pltpu.make_async_copy(out.at[o], out_hbm.at[base_frame + o], sems.at[o]))
        copies[o].start()
    for copy in copies:
        copy.wait()


VMEM = pl.BlockSpec(memory_space=pltpu.VMEM)
HBM = pl.BlockSpec(memory_space=pltpu.MemorySpace.HBM)
PARAMS = pltpu.CompilerParams(vmem_limit_bytes=32 * 1024 * 1024)
DMA = pltpu.SemaphoreType.DMA


def scratch(frames, rows):
    return [
        pltpu.VMEM((3, frames, rows, 128, 128), BF16),
        pltpu.VMEM((36 * 128, 256), BF16),
        pltpu.VMEM((3, 9 * 128, 128), BF16),
    ]


def cost(pairs, rows, more=1):
    positions = pairs * rows * 128
    return pl.CostEstimate(
        flops=2 * positions * 36 * 128 * 256 * more, bytes_accessed=4 << 20, transcendentals=2 * positions * 128
    )


def in_hbm(v):
    return pltpu.with_memory_space_constraint(v, pltpu.MemorySpace.HBM)


def shape(dims, dtype):
    return jax.ShapeDtypeStruct(dims, dtype)


def shards(features, gain_one, shift_one, kernel_one, bias_one, gain_two, shift_two, kernel_two, bias_two):
    slabs = lax.axis_size("tm")
    strips = lax.axis_size("space")
    devices = slabs * strips
    cells = float(4 * 8 * 128 * MEMBERS)
    swap_in = [(i, i ^ 1) for i in range(strips)]
    swap_far = [(i, i + 1) for i in range(1, strips - 1, 2)] + [(i + 1, i) for i in range(1, strips - 1, 2)]
    later = [(i, i + 1) for i in range(slabs - 1)]
    taps_one = kernel_one.reshape(3, 9 * 128, 128)
    taps_two = kernel_two.reshape(3, 9 * 128, 128)

    taps_one, taps_two = in_hbm(taps_one), in_hbm(taps_two)
    x, pay, z_send, in_send, far_send, small = pl.pallas_call(
        stats_kernel,
        out_shape=[
            shape((4, 8, 128, 128), BF16), shape((devices, 128), F32), shape((2, 8, 128, 128), BF16),
            shape((4, 2, 128, 128), BF16), shape((4, 2, 128, 128), BF16), shape((6, 128), F32),
        ],
        in_specs=[HBM] * 7, out_specs=[VMEM] * 6,
        scratch_shapes=[pltpu.VMEM((6, 128), F32), DMA((10,))], compiler_params=PARAMS,
        cost_estimate=pl.CostEstimate(flops=1 << 22, bytes_accessed=1 << 20, transcendentals=0), name="stats",
    )(*map(in_hbm, (features, gain_one, shift_one, bias_one, gain_two, shift_two, bias_two)))
    z_one = lax.ppermute(z_send, "tm", later)
    near = lax.ppermute(in_send, "space", swap_in)
    far = lax.ppermute(far_send, "space", swap_far)
    got = lax.all_to_all(pay, BOTH, 0, 0)
    odd = (lax.axis_index("space") & 1) == 1
    low, high = z_one[:, :2], z_one[:, 6:]
    z_near = lax.ppermute(jnp.where(odd, low, high), "space", swap_in)
    z_far = lax.ppermute(jnp.where(odd, high, low), "space", swap_far)
    inner, pay, send = pl.pallas_call(
        functools.partial(first_kernel, cells, strips),
        out_shape=[shape((4, 10, 128, 128), F32), shape((devices, 128), F32), shape((2, 10, 128, 128), BF16)],
        in_specs=[HBM] + [VMEM] * 8, out_specs=[VMEM] * 3, scratch_shapes=scratch(6, 12) + [DMA],
        compiler_params=PARAMS, cost_estimate=cost(2, 10), name="first",
    )(taps_one, got, small, x, near, far, z_one, z_near, z_far)
    got = lax.all_to_all(pay, BOTH, 0, 0)
    z_two = lax.ppermute(send, "tm", later)
    out_scratch = [pltpu.VMEM((2, 8, 128, 128), F32), DMA, DMA((2,))]
    out = pl.pallas_call(
        functools.partial(second_kernel, False, cells, strips),
        out_shape=shape((4, 8, 128, 128), F32),
        in_specs=[HBM] + [VMEM] * 4, out_specs=HBM, scratch_shapes=scratch(4, 10) + out_scratch,
        compiler_params=PARAMS, cost_estimate=cost(1, 8, LATE), name="second_late",
    )(taps_two, got, small, x, inner)
    return pl.pallas_call(
        functools.partial(second_kernel, True, cells, strips),
        out_shape=shape((4, 8, 128, 128), F32),
        in_specs=[HBM] + [VMEM] * 5 + [HBM], out_specs=HBM, scratch_shapes=scratch(4, 10) + out_scratch,
        input_output_aliases={6: 0}, compiler_params=PARAMS, cost_estimate=cost(1, 8), name="second_early",
    )(taps_two, got, small, x, inner, z_two, out)


def solution(mesh):
    placed = (P("tm", "space", None, None), P(), P(), P(), P(), P(), P(), P(), P())
    return jax.shard_map(
        shards, mesh=mesh, in_specs=placed, out_specs=P("tm", "space", None, None), check_vma=False
    )
```

```python
import functools

import jax
import jax.numpy as jnp
from jax import lax
from jax.experimental import pallas as pl
from jax.experimental.pallas import tpu as pltpu
from jax.sharding import PartitionSpec as P

EPS = 1e-06
MEMBERS = 4
BOTH = ("tm", "space")
F32 = jnp.float32
BF16 = jnp.bfloat16


def lane_of(shape):
    return lax.broadcasted_iota(jnp.int32, shape, len(shape) - 1)


def group_sum(v):
    lane = lane_of(v.shape)
    width = v.shape[-1]
    axis = v.ndim - 1
    v = v + jnp.where((lane & 1) == 1, pltpu.roll(v, 1, axis), pltpu.roll(v, width - 1, axis))
    return v + jnp.where((lane & 2) == 2, pltpu.roll(v, 2, axis), pltpu.roll(v, width - 2, axis))


def column_sum(v):
    return jnp.broadcast_to(jnp.sum(v, axis=0, keepdims=True), (8, v.shape[1]))


def add_up(blocks):
    total = next(blocks)
    for block in blocks:
        total = total + block
    return total


def local_stats(load, rows, cells, total=None):
    if total is None:
        total = add_up(load(i) for i in range(rows))
    mean = group_sum(column_sum(total)) / cells

    def spread(i):
        d = load(i) - mean[:1]
        return d * d

    return mean, group_sum(column_sum(add_up(spread(i) for i in range(rows))))


def payload(*entries):
    place = lane_of(entries[0].shape) & 3
    out = jnp.zeros_like(entries[0])
    for i, entry in enumerate(entries):
        out = jnp.where(place == i, entry, out)
    return out


def pick(rows, place):
    return group_sum(jnp.where((lane_of(rows.shape) & 3) == place, rows, 0.0))


def whole_stats(got_ref, cells):
    got = got_ref[...]
    devices = got.shape[0]
    place = lane_of(got.shape) & 3
    means = jnp.where(place == 0, got, 0.0)
    mean = group_sum(column_sum(means)) / devices
    spread = group_sum(column_sum(jnp.where(place == 1, got, 0.0)))
    off = jnp.where(place == 0, got - mean[:1], 0.0)
    between = group_sum(column_sum(off * off))
    var = (spread + between * cells) / (cells * devices)
    return mean, lax.rsqrt(var + EPS)


def put_act(off, slope, half_shift, keep, out, f, r):
    h = off * slope + half_shift
    y = h + h * jnp.tanh(h)
    if keep is not None:
        y = y * keep
    row = lax.broadcasted_iota(jnp.int32, y.shape, 0)
    out[0, f, r] = jnp.where(row == 0, 0.0, pltpu.roll(y, 1, 0)).astype(BF16)
    out[1, f, r] = y.astype(BF16)
    out[2, f, r] = jnp.where(row == 127, 0.0, pltpu.roll(y, 127, 0)).astype(BF16)


def build_taps(kernel, taps):
    zero = jnp.zeros((9 * 128, 128), BF16)
    for f in range(4):
        at = pl.ds(f * 9 * 128, 9 * 128)
        taps[at, :128] = kernel[f] if f < 3 else zero
        taps[at, 128:] = kernel[f - 1] if f > 0 else zero


def conv_pair(acts, taps, first, at, rows):
    pieces = []
    for f in range(4):
        for i in range(3):
            for j in range(3):
                pieces.append(acts[j, first + f, pl.ds(at + i, rows)].reshape(rows * 128, 128))
    return jnp.dot(jnp.concatenate(pieces, axis=-1), taps[...], preferred_element_type=F32)


def stats_kernel(x_hbm, *refs):
    small, (x_ref, pay_ref, z_ref, in_ref, far_ref, small_ref, sems) = refs[:6], refs[6:]
    frames, per = x_ref.shape[:2]
    copies = [pltpu.make_async_copy(x_hbm.at[f], x_ref.at[f], sems.at[f]) for f in range(frames)]
    copies += [pltpu.make_async_copy(v, small_ref.at[i], sems.at[frames + i]) for i, v in enumerate(small)]
    for copy in copies:
        copy.start()
    odd = (lax.axis_index("space") & 1) == 1
    total = None
    for f in range(frames):
        copies[f].wait()
        part = add_up(x_ref[f, r].astype(F32) for r in range(per))
        total = part if f == 0 else total + part
        for r in range(2):
            low, high = x_ref[f, r], x_ref[f, per - 2 + r]
            in_ref[f, r] = jnp.where(odd, low, high)
            far_ref[f, r] = jnp.where(odd, high, low)
    z_ref[...] = x_ref[2:]
    rows = frames * per
    load = lambda i: x_ref[i // per, i % per].astype(F32)
    mean, spread = local_stats(load, rows, float(rows * 128 * MEMBERS), total)
    pay_ref[...] = jnp.broadcast_to(payload(mean, spread)[:1], pay_ref.shape)
    for copy in copies[frames:]:
        copy.wait()


def norm_constants(got_ref, small_ref, at, cells):
    mean, scale = whole_stats(got_ref, cells)
    gain, shift, bias = (small_ref[at + i : at + i + 1] for i in range(3))
    return mean[:1], scale[:1] * gain * 0.5, shift * 0.5, bias


def edges(strips):
    space = lax.axis_index("space")
    return jnp.where(space == 0, 0.0, 1.0), jnp.where(space == strips - 1, 0.0, 1.0)


def first_kernel(cells, strips, kernel_hbm, got_ref, small_ref, x_ref, in_ref, far_ref,
                 z_ref, z_in_ref, z_far_ref, inner_ref, pay_ref, send_ref, acts, taps, kernel, sem):
    fetch = pltpu.make_async_copy(kernel_hbm, kernel, sem)
    fetch.start()
    mean, slope, half, bias = norm_constants(got_ref, small_ref, 0, cells)
    top, bottom = edges(strips)
    odd = (lax.axis_index("space") & 1) == 1
    start = lax.axis_index("tm") == 0

    def frame(own, near, far, f):
        for r in range(12):
            if 2 <= r < 10:
                x, keep = own(r - 2), None
            else:
                high = r >= 10
                i = r - 10 if high else r
                a, b = near(i), far(i)
                x, keep = (jnp.where(odd, b, a), bottom) if high else (jnp.where(odd, a, b), top)
            put_act(x.astype(F32) - mean, slope, half, keep, acts, f, r)

    def of(ref, f):
        return lambda r: ref[f, r]

    def carried(ref, z, f):
        return lambda r: jnp.where(start, ref[0, r], z[f, r])

    def conv(pair):
        got = conv_pair(acts, taps, 2 * pair, 0, 10)
        for o in range(2):
            inner_ref[2 * pair + o] = (got[:, o * 128 : (o + 1) * 128] + bias).reshape(10, 128, 128)

    for f in range(4):
        if f == 2:
            fetch.wait()
            build_taps(kernel, taps)
        frame(of(x_ref, f), of(in_ref, f), of(far_ref, f), 2 + f)
    def stats(pair):
        return local_stats(lambda i: inner_ref[2 * pair + i // 8, 1 + i % 8], 16, cells / 2)

    conv(1)
    for f in range(2):
        frame(carried(x_ref, z_ref, f), carried(in_ref, z_in_ref, f), carried(far_ref, z_far_ref, f), f)
    late, late_spread = stats(1)
    for o in range(2):
        send_ref[o] = (inner_ref[2 + o] - late[:1]).astype(BF16)
    conv(0)
    early, early_spread = stats(0)
    gap = late - early
    spread = late_spread + early_spread + gap * gap * (cells / 4)
    pay_ref[...] = jnp.broadcast_to(payload((late + early) * 0.5, spread, late)[:1], pay_ref.shape)


def second_kernel(cells, strips, kernel_hbm, got_ref, small_ref, feat_ref, x_ref, z_ref, out_hbm, acts, taps, kernel, out, sem, sems):
    fetch = pltpu.make_async_copy(kernel_hbm, kernel, sem)
    fetch.start()
    mean, slope, half, bias = norm_constants(got_ref, small_ref, 3, cells)
    top, bottom = edges(strips)
    tm = lax.axis_index("tm")
    start = tm == 0
    sender = got_ref[pl.ds(jnp.maximum(tm - 1, 0) * strips + lax.axis_index("space"), 1)]
    base = mean - pick(jnp.broadcast_to(sender, (8, 128)), 2)[:1]

    def frame(off, f):
        for r in range(10):
            put_act(off(r), slope, half, {0: top, 9: bottom}.get(r), acts, f, r)

    copies = []

    def conv(pair, at, rows):
        got = conv_pair(acts, taps, 2 * pair, at, rows)
        for o in range(2):
            f = 2 * pair + o
            part = (got[:, o * 128 : (o + 1) * 128] + bias).reshape(rows, 128, 128)
            out[f, pl.ds(at, rows)] = feat_ref[f, pl.ds(at, rows)].astype(F32) + part
            here = (f, pl.ds(at, rows))
            copies.append(pltpu.make_async_copy(out.at[here], out_hbm.at[here], sems.at[len(copies)]))
            copies[-1].start()

    for f in range(4):
        if f == 2:
            fetch.wait()
            build_taps(kernel, taps)
        frame(lambda r: x_ref[f, r] - mean, 2 + f)
    conv(1, 0, 8)
    for f in range(2):
        frame(lambda r: jnp.where(start, x_ref[0, r] - mean, z_ref[f, r].astype(F32) - base), f)
    for at in (0, 4):
        conv(0, at, 4)
    for copy in copies:
        copy.wait()


VMEM = pl.BlockSpec(memory_space=pltpu.VMEM)
HBM = pl.BlockSpec(memory_space=pltpu.MemorySpace.HBM)
PARAMS = pltpu.CompilerParams(vmem_limit_bytes=32 * 1024 * 1024)
DMA = pltpu.SemaphoreType.DMA


def scratch(frames, rows):
    return [
        pltpu.VMEM((3, frames, rows, 128, 128), BF16),
        pltpu.VMEM((36 * 128, 256), BF16),
        pltpu.VMEM((3, 9 * 128, 128), BF16),
    ]


def cost(pairs, rows):
    positions = pairs * rows * 128
    return pl.CostEstimate(
        flops=2 * positions * 36 * 128 * 256, bytes_accessed=4 << 20, transcendentals=2 * positions * 128
    )


def in_hbm(v):
    return pltpu.with_memory_space_constraint(v, pltpu.MemorySpace.HBM)


def shape(dims, dtype):
    return jax.ShapeDtypeStruct(dims, dtype)


def shards(features, gain_one, shift_one, kernel_one, bias_one, gain_two, shift_two, kernel_two, bias_two):
    slabs = lax.axis_size("tm")
    strips = lax.axis_size("space")
    devices = slabs * strips
    cells = float(4 * 8 * 128 * MEMBERS)
    swap_in = [(i, i ^ 1) for i in range(strips)]
    swap_far = [(i, i + 1) for i in range(1, strips - 1, 2)] + [(i + 1, i) for i in range(1, strips - 1, 2)]
    later = [(i, i + 1) for i in range(slabs - 1)]
    taps_one = kernel_one.reshape(3, 9 * 128, 128)
    taps_two = kernel_two.reshape(3, 9 * 128, 128)

    taps_one, taps_two = in_hbm(taps_one), in_hbm(taps_two)
    x, pay, z_send, in_send, far_send, small = pl.pallas_call(
        stats_kernel,
        out_shape=[
            shape((4, 8, 128, 128), BF16), shape((devices, 128), F32), shape((2, 8, 128, 128), BF16),
            shape((4, 2, 128, 128), BF16), shape((4, 2, 128, 128), BF16), shape((6, 128), F32),
        ],
        in_specs=[HBM] * 7, out_specs=[VMEM] * 6,
        scratch_shapes=[DMA((10,))], compiler_params=PARAMS,
        cost_estimate=pl.CostEstimate(flops=1 << 22, bytes_accessed=1 << 20, transcendentals=0), name="stats",
    )(*map(in_hbm, (features, gain_one, shift_one, bias_one, gain_two, shift_two, bias_two)))
    z_one = lax.ppermute(z_send, "tm", later)
    near = lax.ppermute(in_send, "space", swap_in)
    far = lax.ppermute(far_send, "space", swap_far)
    got = lax.all_to_all(pay, BOTH, 0, 0)
    odd = (lax.axis_index("space") & 1) == 1
    low, high = z_one[:, :2], z_one[:, 6:]
    z_near = lax.ppermute(jnp.where(odd, low, high), "space", swap_in)
    z_far = lax.ppermute(jnp.where(odd, high, low), "space", swap_far)
    inner, pay, send = pl.pallas_call(
        functools.partial(first_kernel, cells, strips),
        out_shape=[shape((4, 10, 128, 128), F32), shape((devices, 128), F32), shape((2, 10, 128, 128), BF16)],
        in_specs=[HBM] + [VMEM] * 8, out_specs=[VMEM] * 3, scratch_shapes=scratch(6, 12) + [DMA],
        compiler_params=PARAMS, cost_estimate=cost(2, 10), name="first",
    )(taps_one, got, small, x, near, far, z_one, z_near, z_far)
    got = lax.all_to_all(pay, BOTH, 0, 0)
    z_two = lax.ppermute(send, "tm", later)
    return pl.pallas_call(
        functools.partial(second_kernel, cells, strips),
        out_shape=shape((4, 8, 128, 128), F32),
        in_specs=[HBM] + [VMEM] * 5, out_specs=HBM,
        scratch_shapes=scratch(6, 10) + [pltpu.VMEM((4, 8, 128, 128), F32), DMA, DMA((6,))],
        compiler_params=PARAMS, cost_estimate=cost(2, 8), name="second",
    )(taps_two, got, small, x, inner, z_two)


def solution(mesh):
    placed = (P("tm", "space", None, None), P(), P(), P(), P(), P(), P(), P(), P())
    return jax.shard_map(
        shards, mesh=mesh, in_specs=placed, out_specs=P("tm", "space", None, None), check_vma=False
    )
```

```python
import functools

import jax
import jax.numpy as jnp
from jax import lax
from jax.experimental import pallas as pl
from jax.experimental.pallas import tpu as pltpu
from jax.sharding import PartitionSpec as P

EPS = 1e-06
MEMBERS = 4
BOTH = ("tm", "space")
F32 = jnp.float32
BF16 = jnp.bfloat16


def lane_of(shape):
    return lax.broadcasted_iota(jnp.int32, shape, len(shape) - 1)


def group_sum(v):
    lane = lane_of(v.shape)
    width = v.shape[-1]
    axis = v.ndim - 1
    v = v + jnp.where((lane & 1) == 1, pltpu.roll(v, 1, axis), pltpu.roll(v, width - 1, axis))
    return v + jnp.where((lane & 2) == 2, pltpu.roll(v, 2, axis), pltpu.roll(v, width - 2, axis))


def column_sum(v):
    return jnp.broadcast_to(jnp.sum(v, axis=0, keepdims=True), (8, v.shape[1]))


def add_up(blocks):
    total = next(blocks)
    for block in blocks:
        total = total + block
    return total


def local_stats(load, rows, cells, total=None):
    if total is None:
        total = add_up(load(i) for i in range(rows))
    mean = group_sum(column_sum(total)) / cells

    def spread(i):
        d = load(i) - mean[:1]
        return d * d

    return mean, group_sum(column_sum(add_up(spread(i) for i in range(rows))))


def shifted_sums(load, rows, shift):
    first = second = None
    for i in range(rows):
        d = load(i) - shift[:1]
        first = d if i == 0 else first + d
        second = d * d if i == 0 else second + d * d
    return group_sum(column_sum(first)), group_sum(column_sum(second))


def joined(mean, spread, cells, first, second, more):
    whole = cells + more
    return mean + first / whole, spread + second - first * first / whole


def payload(*entries):
    place = lane_of(entries[0].shape) & 3
    out = jnp.zeros_like(entries[0])
    for i, entry in enumerate(entries):
        out = jnp.where(place == i, entry, out)
    return out


def pick(rows, place):
    return group_sum(jnp.where((lane_of(rows.shape) & 3) == place, rows, 0.0))


def whole_stats(got_ref, cells):
    got = got_ref[...]
    devices = got.shape[0]
    place = lane_of(got.shape) & 3
    means = jnp.where(place == 0, got, 0.0)
    mean = group_sum(column_sum(means)) / devices
    spread = group_sum(column_sum(jnp.where(place == 1, got, 0.0)))
    off = jnp.where(place == 0, got - mean[:1], 0.0)
    between = group_sum(column_sum(off * off))
    var = (spread + between * cells) / (cells * devices)
    return mean, lax.rsqrt(var + EPS)


def put_act(off, slope, half_shift, keep, out, f, r):
    h = off * slope + half_shift
    y = h + h * jnp.tanh(h)
    if keep is not None:
        y = y * keep
    row = lax.broadcasted_iota(jnp.int32, y.shape, 0)
    out[0, f, r] = jnp.where(row == 0, 0.0, pltpu.roll(y, 1, 0)).astype(BF16)
    out[1, f, r] = y.astype(BF16)
    out[2, f, r] = jnp.where(row == 127, 0.0, pltpu.roll(y, 127, 0)).astype(BF16)


def build_taps(kernel, taps):
    zero = jnp.zeros((9 * 128, 128), BF16)
    for f in range(4):
        at = pl.ds(f * 9 * 128, 9 * 128)
        taps[at, :128] = kernel[f] if f < 3 else zero
        taps[at, 128:] = kernel[f - 1] if f > 0 else zero


def conv_pair(acts, taps, first, at, rows):
    pieces = []
    for f in range(4):
        for i in range(3):
            for j in range(3):
                pieces.append(acts[j, first + f, pl.ds(at + i, rows)].reshape(rows * 128, 128))
    return jnp.dot(jnp.concatenate(pieces, axis=-1), taps[...], preferred_element_type=F32)


def stats_kernel(x_hbm, *refs):
    small, (x_ref, pay_ref, z_ref, in_ref, far_ref, small_ref, sems) = refs[:6], refs[6:]
    frames, per = x_ref.shape[:2]
    copies = [pltpu.make_async_copy(x_hbm.at[f], x_ref.at[f], sems.at[f]) for f in range(frames)]
    copies += [pltpu.make_async_copy(v, small_ref.at[i], sems.at[frames + i]) for i, v in enumerate(small)]
    for copy in copies:
        copy.start()
    odd = (lax.axis_index("space") & 1) == 1
    cells = float(per * 128 * MEMBERS)
    load = lambda i: x_ref[i // per, i % per].astype(F32)
    for f in range(frames):
        copies[f].wait()
        if f == 0:
            mean, spread = local_stats(load, per, cells)
        for r in range(2):
            low, high = x_ref[f, r], x_ref[f, per - 2 + r]
            in_ref[f, r] = jnp.where(odd, low, high)
            far_ref[f, r] = jnp.where(odd, high, low)
    z_ref[...] = x_ref[2:]
    sums = shifted_sums(lambda i: load(per + i), (frames - 1) * per, mean)
    mean, spread = joined(mean, spread, cells, *sums, (frames - 1) * cells)
    pay_ref[...] = jnp.broadcast_to(payload(mean, spread)[:1], pay_ref.shape)
    for copy in copies[frames:]:
        copy.wait()


def norm_constants(got_ref, small_ref, at, cells):
    mean, scale = whole_stats(got_ref, cells)
    gain, shift, bias = (small_ref[at + i : at + i + 1] for i in range(3))
    return mean[:1], scale[:1] * gain * 0.5, shift * 0.5, bias


def edges(strips):
    space = lax.axis_index("space")
    return jnp.where(space == 0, 0.0, 1.0), jnp.where(space == strips - 1, 0.0, 1.0)


def first_kernel(early, cells, strips, *refs):
    if early:
        kernel, consts_ref, small_ref, x_ref, in_ref, far_ref, z_ref, z_in_ref, z_far_ref, inner_ref, pay_ref, acts, taps = refs
        mean, slope, half, late, spread = (consts_ref[i : i + 1] for i in range(5))
        bias = small_ref[2:3]
    else:
        kernel_hbm, got_ref, small_ref, x_ref, in_ref, far_ref, inner_ref, send_ref, consts_ref, kernel, acts, taps, sem = refs
        fetch = pltpu.make_async_copy(kernel_hbm, kernel, sem)
        fetch.start()
        mean, slope, half, bias = norm_constants(got_ref, small_ref, 0, cells)
    top, bottom = edges(strips)
    odd = (lax.axis_index("space") & 1) == 1
    start = lax.axis_index("tm") == 0

    def act(own, near, far, f, r):
        if 2 <= r < 10:
            x, keep = own(r - 2), None
        else:
            high = r >= 10
            i = r - 10 if high else r
            a, b = near(i), far(i)
            x, keep = (jnp.where(odd, b, a), bottom) if high else (jnp.where(odd, a, b), top)
        put_act(x.astype(F32) - mean, slope, half, keep, acts, f, r)

    def of(ref, f):
        return lambda r: ref[f, r]

    def carried(ref, z, f):
        return lambda r: jnp.where(start, ref[0, r], z[f, r])

    if early:
        build_taps(kernel, taps)
        for r in range(12):
            for f in range(2):
                act(carried(x_ref, z_ref, f), carried(in_ref, z_in_ref, f), carried(far_ref, z_far_ref, f), f, r)
                act(of(x_ref, f), of(in_ref, f), of(far_ref, f), 2 + f, r)
    else:
        for f in range(4):
            if f == 2:
                fetch.wait()
                build_taps(kernel, taps)
            for r in range(12):
                act(of(x_ref, f), of(in_ref, f), of(far_ref, f), f, r)
    got = conv_pair(acts, taps, 0, 0, 10)
    for o in range(2):
        inner_ref[o] = (got[:, o * 128 : (o + 1) * 128] + bias).reshape(10, 128, 128)
    own = lambda i: inner_ref[i // 8, 1 + i % 8]
    if early:
        m, spread = joined(late, spread, cells / 2, *shifted_sums(own, 16, late), cells / 2)
        m, spread, late = (jnp.broadcast_to(v[:1], (8, 128)) for v in (m, spread, late))
        pay_ref[...] = jnp.broadcast_to(payload(m, spread, late)[:1], pay_ref.shape)
    else:
        late, spread = local_stats(own, 16, cells / 2)
        for o in range(2):
            send_ref[o] = (inner_ref[o] - late[:1]).astype(BF16)
        for i, v in enumerate((mean, slope, half, late, spread)):
            consts_ref[i : i + 1] = v[:1]


def second_kernel(cells, strips, kernel_ref, got_ref, small_ref, feat_ref, b_ref, a_ref, z_ref, out_hbm, acts, taps, out, sems):
    mean, slope, half, bias = norm_constants(got_ref, small_ref, 3, cells)
    top, bottom = edges(strips)
    tm = lax.axis_index("tm")
    start = tm == 0
    sender = got_ref[pl.ds(jnp.maximum(tm - 1, 0) * strips + lax.axis_index("space"), 1)]
    base = mean - pick(jnp.broadcast_to(sender, (8, 128)), 2)[:1]

    def act(off, f, r):
        put_act(off, slope, half, {0: top, 9: bottom}.get(r), acts, f, r)

    copies = []

    def conv(pair, at, rows):
        got = conv_pair(acts, taps, 2 * pair, at, rows)
        for o in range(2):
            f = 2 * pair + o
            part = (got[:, o * 128 : (o + 1) * 128] + bias).reshape(rows, 128, 128)
            out[f, pl.ds(at, rows)] = feat_ref[f, pl.ds(at, rows)].astype(F32) + part
            here = (f, pl.ds(at, rows))
            copies.append(pltpu.make_async_copy(out.at[here], out_hbm.at[here], sems.at[len(copies)]))
            copies[-1].start()

    build_taps(kernel_ref, taps)
    for r in range(10):
        for f in range(4):
            act((b_ref if f < 2 else a_ref)[f % 2, r] - mean, 2 + f, r)
    conv(1, 0, 8)
    for r in range(10):
        for f in range(2):
            act(jnp.where(start, b_ref[0, r] - mean, z_ref[f, r].astype(F32) - base), f, r)
    for at in (0, 4):
        conv(0, at, 4)
    for copy in copies:
        copy.wait()


VMEM = pl.BlockSpec(memory_space=pltpu.VMEM)
HBM = pl.BlockSpec(memory_space=pltpu.MemorySpace.HBM)
PARAMS = pltpu.CompilerParams(vmem_limit_bytes=32 * 1024 * 1024)
DMA = pltpu.SemaphoreType.DMA


def scratch(frames, rows):
    return [
        pltpu.VMEM((3, frames, rows, 128, 128), BF16),
        pltpu.VMEM((36 * 128, 256), BF16),
    ]


def cost(pairs, rows):
    positions = pairs * rows * 128
    return pl.CostEstimate(
        flops=2 * positions * 36 * 128 * 256, bytes_accessed=4 << 20, transcendentals=2 * positions * 128
    )


def in_hbm(v):
    return pltpu.with_memory_space_constraint(v, pltpu.MemorySpace.HBM)


def shape(dims, dtype):
    return jax.ShapeDtypeStruct(dims, dtype)


def shards(features, gain_one, shift_one, kernel_one, bias_one, gain_two, shift_two, kernel_two, bias_two):
    slabs = lax.axis_size("tm")
    strips = lax.axis_size("space")
    devices = slabs * strips
    cells = float(4 * 8 * 128 * MEMBERS)
    swap_in = [(i, i ^ 1) for i in range(strips)]
    swap_far = [(i, i + 1) for i in range(1, strips - 1, 2)] + [(i + 1, i) for i in range(1, strips - 1, 2)]
    later = [(i, i + 1) for i in range(slabs - 1)]
    taps_one = kernel_one.reshape(3, 9 * 128, 128)
    taps_two = kernel_two.reshape(3, 9 * 128, 128)

    taps_one = in_hbm(taps_one)
    x, pay, z_send, in_send, far_send, small = pl.pallas_call(
        stats_kernel,
        out_shape=[
            shape((4, 8, 128, 128), BF16), shape((devices, 128), F32), shape((2, 8, 128, 128), BF16),
            shape((4, 2, 128, 128), BF16), shape((4, 2, 128, 128), BF16), shape((6, 128), F32),
        ],
        in_specs=[HBM] * 7, out_specs=[VMEM] * 6,
        scratch_shapes=[DMA((10,))], compiler_params=PARAMS,
        cost_estimate=pl.CostEstimate(flops=1 << 22, bytes_accessed=1 << 20, transcendentals=0), name="stats",
    )(*map(in_hbm, (features, gain_one, shift_one, bias_one, gain_two, shift_two, bias_two)))
    z_one = lax.ppermute(z_send, "tm", later)
    near = lax.ppermute(in_send, "space", swap_in)
    far = lax.ppermute(far_send, "space", swap_far)
    got = lax.all_to_all(pay, BOTH, 0, 0)
    odd = (lax.axis_index("space") & 1) == 1
    low, high = z_one[:, :2], z_one[:, 6:]
    z_near = lax.ppermute(jnp.where(odd, low, high), "space", swap_in)
    z_far = lax.ppermute(jnp.where(odd, high, low), "space", swap_far)
    inner_a, send, consts, kernel = pl.pallas_call(
        functools.partial(first_kernel, False, cells, strips),
        out_shape=[shape((2, 10, 128, 128), F32), shape((2, 10, 128, 128), BF16), shape((8, 128), F32), shape((3, 9 * 128, 128), BF16)],
        in_specs=[HBM] + [VMEM] * 5, out_specs=[VMEM] * 4, scratch_shapes=scratch(4, 12) + [DMA],
        compiler_params=PARAMS, cost_estimate=cost(1, 10), name="first_late",
    )(taps_one, got, small, x, near, far)
    z_two = lax.ppermute(send, "tm", later)
    inner_b, pay = pl.pallas_call(
        functools.partial(first_kernel, True, cells, strips),
        out_shape=[shape((2, 10, 128, 128), F32), shape((devices, 128), F32)],
        in_specs=[VMEM] * 9, out_specs=[VMEM] * 2, scratch_shapes=scratch(4, 12),
        compiler_params=PARAMS, cost_estimate=cost(1, 10), name="first_early",
    )(kernel, consts, small, x, near, far, z_one, z_near, z_far)
    got = lax.all_to_all(pay, BOTH, 0, 0)
    return pl.pallas_call(
        functools.partial(second_kernel, cells, strips),
        out_shape=shape((4, 8, 128, 128), F32),
        in_specs=[VMEM] * 7, out_specs=HBM,
        scratch_shapes=scratch(6, 10) + [pltpu.VMEM((4, 8, 128, 128), F32), DMA((6,))],
        compiler_params=PARAMS, cost_estimate=cost(2, 8), name="second",
    )(taps_two, got, small, x, inner_b, inner_a, z_two)


def solution(mesh):
    placed = (P("tm", "space", None, None), P(), P(), P(), P(), P(), P(), P(), P())
    return jax.shard_map(
        shards, mesh=mesh, in_specs=placed, out_specs=P("tm", "space", None, None), check_vma=False
    )
```

```python
import functools

import jax
import jax.numpy as jnp
from jax import lax
from jax.experimental import pallas as pl
from jax.experimental.pallas import tpu as pltpu
from jax.sharding import PartitionSpec as P

EPS = 1e-06
MEMBERS = 4
BOTH = ("tm", "space")
F32 = jnp.float32
BF16 = jnp.bfloat16


def lane_of(shape):
    return lax.broadcasted_iota(jnp.int32, shape, len(shape) - 1)


def group_sum(v):
    lane = lane_of(v.shape)
    width = v.shape[-1]
    axis = v.ndim - 1
    v = v + jnp.where((lane & 1) == 1, pltpu.roll(v, 1, axis), pltpu.roll(v, width - 1, axis))
    return v + jnp.where((lane & 2) == 2, pltpu.roll(v, 2, axis), pltpu.roll(v, width - 2, axis))


def column_sum(v):
    return jnp.broadcast_to(jnp.sum(v, axis=0, keepdims=True), (8, v.shape[1]))


def add_up(blocks):
    total = next(blocks)
    for block in blocks:
        total = total + block
    return total


def local_stats(load, rows, cells, total=None):
    if total is None:
        total = add_up(load(i) for i in range(rows))
    mean = group_sum(column_sum(total)) / cells

    def spread(i):
        d = load(i) - mean[:1]
        return d * d

    return mean, group_sum(column_sum(add_up(spread(i) for i in range(rows))))


def shifted_sums(load, rows, shift):
    first = second = None
    for i in range(rows):
        d = load(i) - shift[:1]
        first = d if i == 0 else first + d
        second = d * d if i == 0 else second + d * d
    return group_sum(column_sum(first)), group_sum(column_sum(second))


def joined(mean, spread, cells, first, second, more):
    whole = cells + more
    return mean + first / whole, spread + second - first * first / whole


def payload(*entries):
    place = lane_of(entries[0].shape) & 3
    out = jnp.zeros_like(entries[0])
    for i, entry in enumerate(entries):
        out = jnp.where(place == i, entry, out)
    return out


def pick(rows, place):
    return group_sum(jnp.where((lane_of(rows.shape) & 3) == place, rows, 0.0))


def whole_stats(got_ref, cells):
    got = got_ref[...]
    devices = got.shape[0]
    place = lane_of(got.shape) & 3
    means = jnp.where(place == 0, got, 0.0)
    mean = group_sum(column_sum(means)) / devices
    spread = group_sum(column_sum(jnp.where(place == 1, got, 0.0)))
    off = jnp.where(place == 0, got - mean[:1], 0.0)
    between = group_sum(column_sum(off * off))
    var = (spread + between * cells) / (cells * devices)
    return mean, lax.rsqrt(var + EPS)


def put_act(off, slope, half_shift, keep, out, f, r):
    h = off * slope + half_shift
    y = h + h * jnp.tanh(h)
    if keep is not None:
        y = y * keep
    out[f, r] = y.astype(BF16)


def build_taps(kernel, mid, side):
    zero = jnp.zeros((128, 128), BF16)
    tap = lambda a, i, j: kernel[a, (3 * i + j) * 128 : (3 * i + j + 1) * 128]
    for f in range(4):
        for i in range(3):
            at = pl.ds((3 * f + i) * 128, 128)
            mid[at, :128] = tap(f, i, 1) if f < 3 else zero
            mid[at, 128:] = tap(f - 1, i, 1) if f > 0 else zero
            if f < 3:
                side[at, :128] = tap(f, i, 0)
                side[at, 128:] = tap(f, i, 2)


def conv_pair(acts, mid, side, first, at, rows, put):
    pieces = [[acts[first + f, pl.ds(at + i, rows)].reshape(rows * 128, 128) for i in range(3)] for f in range(4)]
    dot = lambda blocks, taps: jnp.dot(jnp.concatenate(blocks, axis=-1), taps[...], preferred_element_type=F32)
    centre = dot(sum(pieces, []), mid)
    col = lax.broadcasted_iota(jnp.int32, (128, 128), 0)
    for o in range(2):
        sides = dot(sum(pieces[o : o + 3], []), side)
        for r in range(rows):
            here = slice(r * 128, (r + 1) * 128)
            left = jnp.where(col == 0, 0.0, pltpu.roll(sides[here, :128], 1, 0))
            right = jnp.where(col == 127, 0.0, pltpu.roll(sides[here, 128:], 127, 0))
            put(o, at + r, centre[here, o * 128 : (o + 1) * 128] + left + right)


def stats_kernel(x_hbm, *refs):
    small, (x_ref, pay_ref, z_ref, in_ref, far_ref, small_ref, sems) = refs[:6], refs[6:]
    frames, per = x_ref.shape[:2]
    copies = [pltpu.make_async_copy(x_hbm.at[f], x_ref.at[f], sems.at[f]) for f in range(frames)]
    copies += [pltpu.make_async_copy(v, small_ref.at[i], sems.at[frames + i]) for i, v in enumerate(small)]
    for copy in copies:
        copy.start()
    odd = (lax.axis_index("space") & 1) == 1
    cells = float(per * 128 * MEMBERS)
    load = lambda i: x_ref[i // per, i % per].astype(F32)
    for f in range(frames):
        copies[f].wait()
        if f == 0:
            mean, spread = local_stats(load, per, cells)
        for r in range(2):
            low, high = x_ref[f, r], x_ref[f, per - 2 + r]
            in_ref[f, r] = jnp.where(odd, low, high)
            far_ref[f, r] = jnp.where(odd, high, low)
    z_ref[...] = x_ref[2:]
    sums = shifted_sums(lambda i: load(per + i), (frames - 1) * per, mean)
    mean, spread = joined(mean, spread, cells, *sums, (frames - 1) * cells)
    pay_ref[...] = jnp.broadcast_to(payload(mean, spread)[:1], pay_ref.shape)
    for copy in copies[frames:]:
        copy.wait()


def pack_kernel(z_ref, near_ref, far_ref):
    per = z_ref.shape[1]
    odd = lax.axis_index("space") & 1
    for f in range(2):
        near_ref[f] = z_ref[f, pl.ds((1 - odd) * (per - 2), 2)]
        far_ref[f] = z_ref[f, pl.ds(odd * (per - 2), 2)]


def norm_constants(got_ref, small_ref, at, cells):
    mean, scale = whole_stats(got_ref, cells)
    gain, shift, bias = (small_ref[at + i : at + i + 1] for i in range(3))
    return mean[:1], scale[:1] * gain * 0.5, shift * 0.5, bias


def edges(strips):
    space = lax.axis_index("space")
    return jnp.where(space == 0, 0.0, 1.0), jnp.where(space == strips - 1, 0.0, 1.0)


def first_kernel(early, cells, strips, *refs):
    if early:
        kernel, consts_ref, small_ref, x_ref, in_ref, far_ref, z_ref, z_in_ref, z_far_ref, inner_ref, pay_ref, acts, mid, side = refs
        mean, slope, half, late, spread = (consts_ref[i : i + 1] for i in range(5))
        bias = small_ref[2:3]
    else:
        kernel_hbm, got_ref, small_ref, x_ref, in_ref, far_ref, inner_ref, send_ref, consts_ref, kernel, acts, mid, side, sem = refs
        fetch = pltpu.make_async_copy(kernel_hbm, kernel, sem)
        fetch.start()
        mean, slope, half, bias = norm_constants(got_ref, small_ref, 0, cells)
    top, bottom = edges(strips)
    odd = (lax.axis_index("space") & 1) == 1
    start = lax.axis_index("tm") == 0

    def act(own, near, far, f, r):
        if 2 <= r < 10:
            x, keep = own(r - 2), None
        else:
            high = r >= 10
            i = r - 10 if high else r
            a, b = near(i), far(i)
            x, keep = (jnp.where(odd, b, a), bottom) if high else (jnp.where(odd, a, b), top)
        put_act(x.astype(F32) - mean, slope, half, keep, acts, f, r)

    def of(ref, f):
        return lambda r: ref[f, r]

    def carried(ref, z, f):
        return lambda r: jnp.where(start, ref[0, r], z[f, r])

    if early:
        build_taps(kernel, mid, side)
        for r in range(12):
            for f in range(2):
                act(carried(x_ref, z_ref, f), carried(in_ref, z_in_ref, f), carried(far_ref, z_far_ref, f), f, r)
                act(of(x_ref, f), of(in_ref, f), of(far_ref, f), 2 + f, r)
    else:
        for f in range(4):
            if f == 2:
                fetch.wait()
                build_taps(kernel, mid, side)
            for r in range(12):
                act(of(x_ref, f), of(in_ref, f), of(far_ref, f), f, r)

    def put(o, r, value):
        inner_ref[o, r] = value + bias

    conv_pair(acts, mid, side, 0, 0, 10, put)
    own = lambda i: inner_ref[i // 8, 1 + i % 8]
    if early:
        m, spread = joined(late, spread, cells / 2, *shifted_sums(own, 16, late), cells / 2)
        m, spread, late = (jnp.broadcast_to(v[:1], (8, 128)) for v in (m, spread, late))
        pay_ref[...] = jnp.broadcast_to(payload(m, spread, late)[:1], pay_ref.shape)
    else:
        late, spread = local_stats(own, 16, cells / 2)
        for o in range(2):
            send_ref[o] = (inner_ref[o] - late[:1]).astype(BF16)
        for i, v in enumerate((mean, slope, half, late, spread)):
            consts_ref[i : i + 1] = v[:1]


def second_kernel(cells, strips, kernel_ref, got_ref, small_ref, feat_ref, b_ref, a_ref, z_ref, out_hbm, acts, mid, side, out, sems):
    mean, slope, half, bias = norm_constants(got_ref, small_ref, 3, cells)
    top, bottom = edges(strips)
    tm = lax.axis_index("tm")
    start = tm == 0
    sender = got_ref[pl.ds(jnp.maximum(tm - 1, 0) * strips + lax.axis_index("space"), 1)]
    base = mean - pick(jnp.broadcast_to(sender, (8, 128)), 2)[:1]

    def act(off, f, r):
        put_act(off, slope, half, {0: top, 9: bottom}.get(r), acts, f, r)

    copies = []

    def conv(pair, at, rows):
        def put(o, r, value):
            f = 2 * pair + o
            out[f, r] = feat_ref[f, r].astype(F32) + (value + bias)

        conv_pair(acts, mid, side, 2 * pair, at, rows, put)
        for o in range(2):
            f = 2 * pair + o
            here = (f, pl.ds(at, rows))
            copies.append(pltpu.make_async_copy(out.at[here], out_hbm.at[here], sems.at[len(copies)]))
            copies[-1].start()

    build_taps(kernel_ref, mid, side)
    for r in range(10):
        for f in range(4):
            act((b_ref if f < 2 else a_ref)[f % 2, r] - mean, 2 + f, r)
    conv(1, 0, 8)
    for r in range(10):
        for f in range(2):
            act(jnp.where(start, b_ref[0, r] - mean, z_ref[f, r].astype(F32) - base), f, r)
    for at in (0, 4):
        conv(0, at, 4)
    for copy in copies:
        copy.wait()


VMEM = pl.BlockSpec(memory_space=pltpu.VMEM)
HBM = pl.BlockSpec(memory_space=pltpu.MemorySpace.HBM)
PARAMS = pltpu.CompilerParams(vmem_limit_bytes=32 * 1024 * 1024)
DMA = pltpu.SemaphoreType.DMA


def scratch(frames, rows):
    return [
        pltpu.VMEM((frames, rows, 128, 128), BF16),
        pltpu.VMEM((12 * 128, 256), BF16),
        pltpu.VMEM((9 * 128, 256), BF16),
    ]


def cost(pairs, rows):
    positions = pairs * rows * 128
    return pl.CostEstimate(
        flops=2 * positions * 36 * 128 * 256, bytes_accessed=4 << 20, transcendentals=2 * positions * 128
    )


def in_hbm(v):
    return pltpu.with_memory_space_constraint(v, pltpu.MemorySpace.HBM)


def shape(dims, dtype):
    return jax.ShapeDtypeStruct(dims, dtype)


def shards(features, gain_one, shift_one, kernel_one, bias_one, gain_two, shift_two, kernel_two, bias_two):
    slabs = lax.axis_size("tm")
    strips = lax.axis_size("space")
    devices = slabs * strips
    cells = float(4 * 8 * 128 * MEMBERS)
    swap_in = [(i, i ^ 1) for i in range(strips)]
    swap_far = [(i, i + 1) for i in range(1, strips - 1, 2)] + [(i + 1, i) for i in range(1, strips - 1, 2)]
    later = [(i, i + 1) for i in range(slabs - 1)]
    taps_one = kernel_one.reshape(3, 9 * 128, 128)
    taps_two = kernel_two.reshape(3, 9 * 128, 128)

    taps_one = in_hbm(taps_one)
    x, pay, z_send, in_send, far_send, small = pl.pallas_call(
        stats_kernel,
        out_shape=[
            shape((4, 8, 128, 128), BF16), shape((devices, 128), F32), shape((2, 8, 128, 128), BF16),
            shape((4, 2, 128, 128), BF16), shape((4, 2, 128, 128), BF16), shape((6, 128), F32),
        ],
        in_specs=[HBM] * 7, out_specs=[VMEM] * 6,
        scratch_shapes=[DMA((10,))], compiler_params=PARAMS,
        cost_estimate=pl.CostEstimate(flops=1 << 22, bytes_accessed=1 << 20, transcendentals=0), name="stats",
    )(*map(in_hbm, (features, gain_one, shift_one, bias_one, gain_two, shift_two, bias_two)))
    z_one = lax.ppermute(z_send, "tm", later)
    near = lax.ppermute(in_send, "space", swap_in)
    far = lax.ppermute(far_send, "space", swap_far)
    got = lax.all_to_all(pay, BOTH, 0, 0)
    near_send, far_send = pl.pallas_call(
        pack_kernel, out_shape=[shape((2, 2, 128, 128), BF16)] * 2, in_specs=[VMEM], out_specs=[VMEM] * 2, compiler_params=PARAMS,
        cost_estimate=pl.CostEstimate(flops=0, bytes_accessed=1 << 19, transcendentals=0), name="pack",
    )(z_one)
    z_near = lax.ppermute(near_send, "space", swap_in)
    z_far = lax.ppermute(far_send, "space", swap_far)
    inner_a, send, consts, kernel = pl.pallas_call(
        functools.partial(first_kernel, False, cells, strips),
        out_shape=[shape((2, 10, 128, 128), F32), shape((2, 10, 128, 128), BF16), shape((8, 128), F32), shape((3, 9 * 128, 128), BF16)],
        in_specs=[HBM] + [VMEM] * 5, out_specs=[VMEM] * 4, scratch_shapes=scratch(4, 12) + [DMA],
        compiler_params=PARAMS, cost_estimate=cost(1, 10), name="first_late",
    )(taps_one, got, small, x, near, far)
    z_two = lax.ppermute(send, "tm", later)
    inner_b, pay = pl.pallas_call(
        functools.partial(first_kernel, True, cells, strips),
        out_shape=[shape((2, 10, 128, 128), F32), shape((devices, 128), F32)],
        in_specs=[VMEM] * 9, out_specs=[VMEM] * 2, scratch_shapes=scratch(4, 12),
        compiler_params=PARAMS, cost_estimate=cost(1, 10), name="first_early",
    )(kernel, consts, small, x, near, far, z_one, z_near, z_far)
    got = lax.all_to_all(pay, BOTH, 0, 0)
    return pl.pallas_call(
        functools.partial(second_kernel, cells, strips),
        out_shape=shape((4, 8, 128, 128), F32),
        in_specs=[VMEM] * 7, out_specs=HBM,
        scratch_shapes=scratch(6, 10) + [pltpu.VMEM((4, 8, 128, 128), F32), DMA((6,))],
        compiler_params=PARAMS, cost_estimate=cost(2, 8), name="second",
    )(taps_two, got, small, x, inner_b, inner_a, z_two)


def solution(mesh):
    placed = (P("tm", "space", None, None), P(), P(), P(), P(), P(), P(), P(), P())
    return jax.shard_map(
        shards, mesh=mesh, in_specs=placed, out_specs=P("tm", "space", None, None), check_vma=False
    )
```

```python
import functools

import jax
import jax.numpy as jnp
from jax import lax
from jax.experimental import pallas as pl
from jax.experimental.pallas import tpu as pltpu
from jax.sharding import PartitionSpec as P

EPS = 1e-06
MEMBERS = 4
BOTH = ("tm", "space")
F32 = jnp.float32
BF16 = jnp.bfloat16


def lane_of(shape):
    return lax.broadcasted_iota(jnp.int32, shape, len(shape) - 1)


def group_sum(v):
    lane = lane_of(v.shape)
    width = v.shape[-1]
    axis = v.ndim - 1
    v = v + jnp.where((lane & 1) == 1, pltpu.roll(v, 1, axis), pltpu.roll(v, width - 1, axis))
    return v + jnp.where((lane & 2) == 2, pltpu.roll(v, 2, axis), pltpu.roll(v, width - 2, axis))


def column_sum(v):
    return jnp.broadcast_to(jnp.sum(v, axis=0, keepdims=True), (8, v.shape[1]))


def add_up(blocks):
    total = next(blocks)
    for block in blocks:
        total = total + block
    return total


def local_stats(load, rows, cells, total=None):
    if total is None:
        total = add_up(load(i) for i in range(rows))
    mean = group_sum(column_sum(total)) / cells

    def spread(i):
        d = load(i) - mean[:1]
        return d * d

    return mean, group_sum(column_sum(add_up(spread(i) for i in range(rows))))


def shifted_sums(load, rows, shift):
    first = second = None
    for i in range(rows):
        d = load(i) - shift[:1]
        first = d if i == 0 else first + d
        second = d * d if i == 0 else second + d * d
    return group_sum(column_sum(first)), group_sum(column_sum(second))


def joined(mean, spread, cells, first, second, more):
    whole = cells + more
    return mean + first / whole, spread + second - first * first / whole


def payload(*entries):
    place = lane_of(entries[0].shape) & 3
    out = jnp.zeros_like(entries[0])
    for i, entry in enumerate(entries):
        out = jnp.where(place == i, entry, out)
    return out


def pick(rows, place):
    return group_sum(jnp.where((lane_of(rows.shape) & 3) == place, rows, 0.0))


def whole_stats(got_ref, cells):
    got = got_ref[...]
    devices = got.shape[0]
    place = lane_of(got.shape) & 3
    off = got - got[:1]
    sums = jnp.where(place == 0, off, jnp.where(place == 1, got, 0.0))
    sums = column_sum(sums)
    squares = group_sum(column_sum(jnp.where(place == 0, off * off, 0.0)))
    here = lane_of(sums.shape) & 3
    shift = group_sum(jnp.where(here == 0, sums, 0.0)) / devices
    spread = group_sum(jnp.where(here == 1, sums, 0.0))
    first = group_sum(jnp.where(here == 0, jnp.broadcast_to(got[:1], sums.shape), 0.0))
    var = spread / (cells * devices) + (squares / devices - shift * shift)
    return first + shift, lax.rsqrt(var + EPS)


def put_act(off, slope, half_shift, keep, out, f, r):
    h = off * slope + half_shift
    y = h + h * jnp.tanh(h)
    if keep is not None:
        y = y * keep
    out[f, r] = y.astype(BF16)


def build_taps(kernel, mid, side):
    zero = jnp.zeros((128, 128), BF16)
    tap = lambda a, i, j: kernel[a, (3 * i + j) * 128 : (3 * i + j + 1) * 128]
    for f in range(4):
        for i in range(3):
            at = pl.ds((3 * f + i) * 128, 128)
            mid[at, :128] = tap(f, i, 1) if f < 3 else zero
            mid[at, 128:] = tap(f - 1, i, 1) if f > 0 else zero
            if f < 3:
                side[at, :128] = tap(f, i, 0)
                side[at, 128:] = tap(f, i, 2)


def conv_pair(acts, mid, side, first, at, rows, put):
    pieces = [[acts[first + f, pl.ds(at + i, rows)].reshape(rows * 128, 128) for i in range(3)] for f in range(4)]
    dot = lambda blocks, taps: jnp.dot(jnp.concatenate(blocks, axis=-1), taps[...], preferred_element_type=F32)
    centre = dot(sum(pieces, []), mid)
    col = lax.broadcasted_iota(jnp.int32, (128, 128), 0)
    for o in range(2):
        sides = dot(sum(pieces[o : o + 3], []), side)
        for r in range(rows):
            here = slice(r * 128, (r + 1) * 128)
            left = jnp.where(col == 0, 0.0, pltpu.roll(sides[here, :128], 1, 0))
            right = jnp.where(col == 127, 0.0, pltpu.roll(sides[here, 128:], 127, 0))
            put(o, at + r, centre[here, o * 128 : (o + 1) * 128] + left + right)


def stats_kernel(x_hbm, *refs):
    small, (x_ref, pay_ref, z_ref, in_ref, far_ref, small_ref, sems) = refs[:6], refs[6:]
    frames, per = x_ref.shape[:2]
    copies = [pltpu.make_async_copy(x_hbm.at[f], x_ref.at[f], sems.at[f]) for f in range(frames)]
    copies += [pltpu.make_async_copy(v, small_ref.at[i], sems.at[frames + i]) for i, v in enumerate(small)]
    for copy in copies:
        copy.start()
    odd = (lax.axis_index("space") & 1) == 1
    cells = float(per * 128 * MEMBERS)
    load = lambda i: x_ref[i // per, i % per].astype(F32)
    for f in range(frames):
        copies[f].wait()
        if f == 0:
            mean, spread = local_stats(load, per, cells)
        for r in range(2):
            low, high = x_ref[f, r], x_ref[f, per - 2 + r]
            in_ref[f, r] = jnp.where(odd, low, high)
            far_ref[f, r] = jnp.where(odd, high, low)
    z_ref[...] = x_ref[2:]
    sums = shifted_sums(lambda i: load(per + i), (frames - 1) * per, mean)
    mean, spread = joined(mean, spread, cells, *sums, (frames - 1) * cells)
    pay_ref[...] = jnp.broadcast_to(payload(mean, spread)[:1], pay_ref.shape)
    for copy in copies[frames:]:
        copy.wait()


def pack_kernel(z_ref, near_ref, far_ref):
    per = z_ref.shape[1]
    odd = lax.axis_index("space") & 1
    for f in range(2):
        near_ref[f] = z_ref[f, pl.ds((1 - odd) * (per - 2), 2)]
        far_ref[f] = z_ref[f, pl.ds(odd * (per - 2), 2)]


def norm_constants(got_ref, small_ref, at, cells):
    mean, scale = whole_stats(got_ref, cells)
    gain, shift, bias = (small_ref[at + i : at + i + 1] for i in range(3))
    return mean[:1], scale[:1] * gain * 0.5, shift * 0.5, bias


def edges(strips):
    space = lax.axis_index("space")
    return jnp.where(space == 0, 0.0, 1.0), jnp.where(space == strips - 1, 0.0, 1.0)


def first_kernel(early, cells, strips, *refs):
    if early:
        kernel, consts_ref, small_ref, x_ref, in_ref, far_ref, z_ref, z_in_ref, z_far_ref, inner_ref, pay_ref, acts, mid, side = refs
        mean, slope, half, late, spread = (consts_ref[i : i + 1] for i in range(5))
        bias = small_ref[2:3]
    else:
        kernel_hbm, got_ref, small_ref, x_ref, in_ref, far_ref, inner_ref, send_ref, consts_ref, kernel, acts, mid, side, sem = refs
        fetch = pltpu.make_async_copy(kernel_hbm, kernel, sem)
        fetch.start()
        mean, slope, half, bias = norm_constants(got_ref, small_ref, 0, cells)
    top, bottom = edges(strips)
    odd = (lax.axis_index("space") & 1) == 1
    start = lax.axis_index("tm") == 0

    def act(own, near, far, f, r):
        if 2 <= r < 10:
            x, keep = own(r - 2), None
        else:
            high = r >= 10
            i = r - 10 if high else r
            a, b = near(i), far(i)
            x, keep = (jnp.where(odd, b, a), bottom) if high else (jnp.where(odd, a, b), top)
        put_act(x.astype(F32) - mean, slope, half, keep, acts, f, r)

    def of(ref, f):
        return lambda r: ref[f, r]

    def carried(ref, z, f):
        return lambda r: jnp.where(start, ref[0, r], z[f, r])

    def put(o, r, value):
        inner_ref[o, r] = value + bias

    done = 0
    for at, rows in (((0, 6), (6, 4)) if early else ((0, 5), (5, 5))):
        for r in range(done, at + rows + 2):
            for f in range(2):
                if early:
                    act(carried(x_ref, z_ref, f), carried(in_ref, z_in_ref, f), carried(far_ref, z_far_ref, f), f, r)
                    act(of(x_ref, f), of(in_ref, f), of(far_ref, f), 2 + f, r)
                else:
                    act(of(x_ref, 2 * f), of(in_ref, 2 * f), of(far_ref, 2 * f), 2 * f, r)
                    act(of(x_ref, 2 * f + 1), of(in_ref, 2 * f + 1), of(far_ref, 2 * f + 1), 2 * f + 1, r)
        done = at + rows + 2
        if at == 0:
            if not early:
                fetch.wait()
            build_taps(kernel, mid, side)
        conv_pair(acts, mid, side, 0, at, rows, put)
    own = lambda i: inner_ref[i // 8, 1 + i % 8]
    if early:
        m, spread = joined(late, spread, cells / 2, *shifted_sums(own, 16, late), cells / 2)
        m, spread, late = (jnp.broadcast_to(v[:1], (8, 128)) for v in (m, spread, late))
        pay_ref[...] = jnp.broadcast_to(payload(m, spread, late)[:1], pay_ref.shape)
    else:
        late, spread = local_stats(own, 16, cells / 2)
        for o in range(2):
            send_ref[o] = (inner_ref[o] - late[:1]).astype(BF16)
        for i, v in enumerate((mean, slope, half, late, spread)):
            consts_ref[i : i + 1] = v[:1]


def second_kernel(cells, strips, kernel_ref, got_ref, small_ref, feat_ref, b_ref, a_ref, z_ref, out_hbm, acts, mid, side, out, sems):
    mean, slope, half, bias = norm_constants(got_ref, small_ref, 3, cells)
    top, bottom = edges(strips)
    tm = lax.axis_index("tm")
    start = tm == 0
    sender = got_ref[pl.ds(jnp.maximum(tm - 1, 0) * strips + lax.axis_index("space"), 1)]
    base = mean - pick(jnp.broadcast_to(sender, (8, 128)), 2)[:1]

    def act(off, f, r):
        put_act(off, slope, half, {0: top, 9: bottom}.get(r), acts, f, r)

    copies = []

    def conv(pair, at, rows):
        def put(o, r, value):
            f = 2 * pair + o
            out[f, r] = feat_ref[f, r].astype(F32) + (value + bias)

        conv_pair(acts, mid, side, 2 * pair, at, rows, put)
        for o in range(2):
            f = 2 * pair + o
            here = (f, pl.ds(at, rows))
            copies.append(pltpu.make_async_copy(out.at[here], out_hbm.at[here], sems.at[len(copies)]))
            copies[-1].start()

    build_taps(kernel_ref, mid, side)
    for pair, chunks in ((1, ((0, 4), (4, 4))), (0, ((0, 5), (5, 3)))):
        done = 0
        for at, rows in chunks:
            for r in range(done, at + rows + 2):
                for f in range(4 if pair else 2):
                    if pair:
                        act((b_ref if f < 2 else a_ref)[f % 2, r] - mean, 2 + f, r)
                    else:
                        act(jnp.where(start, b_ref[0, r] - mean, z_ref[f, r].astype(F32) - base), f, r)
            done = at + rows + 2
            conv(pair, at, rows)
    for copy in copies:
        copy.wait()


VMEM = pl.BlockSpec(memory_space=pltpu.VMEM)
HBM = pl.BlockSpec(memory_space=pltpu.MemorySpace.HBM)
PARAMS = pltpu.CompilerParams(vmem_limit_bytes=32 * 1024 * 1024)
DMA = pltpu.SemaphoreType.DMA


def scratch(frames, rows):
    return [
        pltpu.VMEM((frames, rows, 128, 128), BF16),
        pltpu.VMEM((12 * 128, 256), BF16),
        pltpu.VMEM((9 * 128, 256), BF16),
    ]


def cost(pairs, rows):
    positions = pairs * rows * 128
    return pl.CostEstimate(
        flops=2 * positions * 36 * 128 * 256, bytes_accessed=4 << 20, transcendentals=2 * positions * 128
    )


def in_hbm(v):
    return pltpu.with_memory_space_constraint(v, pltpu.MemorySpace.HBM)


def shape(dims, dtype):
    return jax.ShapeDtypeStruct(dims, dtype)


def shards(features, gain_one, shift_one, kernel_one, bias_one, gain_two, shift_two, kernel_two, bias_two):
    slabs = lax.axis_size("tm")
    strips = lax.axis_size("space")
    devices = slabs * strips
    cells = float(4 * 8 * 128 * MEMBERS)
    swap_in = [(i, i ^ 1) for i in range(strips)]
    swap_far = [(i, i + 1) for i in range(1, strips - 1, 2)] + [(i + 1, i) for i in range(1, strips - 1, 2)]
    later = [(i, i + 1) for i in range(slabs - 1)]
    taps_one = kernel_one.reshape(3, 9 * 128, 128)
    taps_two = kernel_two.reshape(3, 9 * 128, 128)

    taps_one = in_hbm(taps_one)
    x, pay, z_send, in_send, far_send, small = pl.pallas_call(
        stats_kernel,
        out_shape=[
            shape((4, 8, 128, 128), BF16), shape((devices, 128), F32), shape((2, 8, 128, 128), BF16),
            shape((4, 2, 128, 128), BF16), shape((4, 2, 128, 128), BF16), shape((6, 128), F32),
        ],
        in_specs=[HBM] * 7, out_specs=[VMEM] * 6,
        scratch_shapes=[DMA((10,))], compiler_params=PARAMS,
        cost_estimate=pl.CostEstimate(flops=1 << 22, bytes_accessed=1 << 20, transcendentals=0), name="stats",
    )(*map(in_hbm, (features, gain_one, shift_one, bias_one, gain_two, shift_two, bias_two)))
    z_one = lax.ppermute(z_send, "tm", later)
    near = lax.ppermute(in_send, "space", swap_in)
    far = lax.ppermute(far_send, "space", swap_far)
    got = lax.all_to_all(pay, BOTH, 0, 0)
    near_send, far_send = pl.pallas_call(
        pack_kernel, out_shape=[shape((2, 2, 128, 128), BF16)] * 2, in_specs=[VMEM], out_specs=[VMEM] * 2, compiler_params=PARAMS,
        cost_estimate=pl.CostEstimate(flops=0, bytes_accessed=1 << 19, transcendentals=0), name="pack",
    )(z_one)
    z_near = lax.ppermute(near_send, "space", swap_in)
    z_far = lax.ppermute(far_send, "space", swap_far)
    inner_a, send, consts, kernel = pl.pallas_call(
        functools.partial(first_kernel, False, cells, strips),
        out_shape=[shape((2, 10, 128, 128), F32), shape((2, 10, 128, 128), BF16), shape((8, 128), F32), shape((3, 9 * 128, 128), BF16)],
        in_specs=[HBM] + [VMEM] * 5, out_specs=[VMEM] * 4, scratch_shapes=scratch(4, 12) + [DMA],
        compiler_params=PARAMS, cost_estimate=cost(1, 10), name="first_late",
    )(taps_one, got, small, x, near, far)
    z_two = lax.ppermute(send, "tm", later)
    inner_b, pay = pl.pallas_call(
        functools.partial(first_kernel, True, cells, strips),
        out_shape=[shape((2, 10, 128, 128), F32), shape((devices, 128), F32)],
        in_specs=[VMEM] * 9, out_specs=[VMEM] * 2, scratch_shapes=scratch(4, 12),
        compiler_params=PARAMS, cost_estimate=cost(1, 10), name="first_early",
    )(kernel, consts, small, x, near, far, z_one, z_near, z_far)
    got = lax.all_to_all(pay, BOTH, 0, 0)
    return pl.pallas_call(
        functools.partial(second_kernel, cells, strips),
        out_shape=shape((4, 8, 128, 128), F32),
        in_specs=[VMEM] * 7, out_specs=HBM,
        scratch_shapes=scratch(6, 10) + [pltpu.VMEM((4, 8, 128, 128), F32), DMA((8,))],
        compiler_params=PARAMS, cost_estimate=cost(2, 8), name="second",
    )(taps_two, got, small, x, inner_b, inner_a, z_two)


def solution(mesh):
    placed = (P("tm", "space", None, None), P(), P(), P(), P(), P(), P(), P(), P())
    return jax.shard_map(
        shards, mesh=mesh, in_specs=placed, out_specs=P("tm", "space", None, None), check_vma=False
    )
```

```python
import functools

import jax
import jax.numpy as jnp
from jax import lax
from jax.experimental import pallas as pl
from jax.experimental.pallas import tpu as pltpu
from jax.sharding import PartitionSpec as P

EPS = 1e-06
MEMBERS = 4
BOTH = ("tm", "space")
F32 = jnp.float32
BF16 = jnp.bfloat16


def lane_of(shape):
    return lax.broadcasted_iota(jnp.int32, shape, len(shape) - 1)


def group_sum(v):
    lane = lane_of(v.shape)
    width = v.shape[-1]
    axis = v.ndim - 1
    v = v + jnp.where((lane & 1) == 1, pltpu.roll(v, 1, axis), pltpu.roll(v, width - 1, axis))
    return v + jnp.where((lane & 2) == 2, pltpu.roll(v, 2, axis), pltpu.roll(v, width - 2, axis))


def column_sum(v):
    return jnp.broadcast_to(jnp.sum(v, axis=0, keepdims=True), (8, v.shape[1]))


def add_up(blocks):
    total = next(blocks)
    for block in blocks:
        total = total + block
    return total


def local_stats(load, rows, cells, total=None):
    if total is None:
        total = add_up(load(i) for i in range(rows))
    mean = group_sum(column_sum(total)) / cells

    def spread(i):
        d = load(i) - mean[:1]
        return d * d

    return mean, group_sum(column_sum(add_up(spread(i) for i in range(rows))))


def shifted_sums(load, rows, shift):
    first = second = None
    for i in range(rows):
        d = load(i) - shift[:1]
        first = d if i == 0 else first + d
        second = d * d if i == 0 else second + d * d
    return group_sum(column_sum(first)), group_sum(column_sum(second))


def joined(mean, spread, cells, first, second, more):
    whole = cells + more
    return mean + first / whole, spread + second - first * first / whole


def payload(*entries):
    place = lane_of(entries[0].shape) & 3
    out = jnp.zeros_like(entries[0])
    for i, entry in enumerate(entries):
        out = jnp.where(place == i, entry, out)
    return out


def pick(rows, place):
    return group_sum(jnp.where((lane_of(rows.shape) & 3) == place, rows, 0.0))


def whole_stats(got_ref, cells):
    got = got_ref[...]
    devices = got.shape[0]
    place = lane_of(got.shape) & 3
    off = got - got[:1]
    sums = jnp.where(place == 0, off, jnp.where(place == 1, got, 0.0))
    sums = column_sum(sums)
    squares = group_sum(column_sum(jnp.where(place == 0, off * off, 0.0)))
    here = lane_of(sums.shape) & 3
    shift = group_sum(jnp.where(here == 0, sums, 0.0)) / devices
    spread = group_sum(jnp.where(here == 1, sums, 0.0))
    first = group_sum(jnp.where(here == 0, jnp.broadcast_to(got[:1], sums.shape), 0.0))
    var = spread / (cells * devices) + (squares / devices - shift * shift)
    return first + shift, lax.rsqrt(var + EPS)


def put_act(off, slope, half_shift, keep, out, f, r):
    h = off * slope + half_shift
    y = h + h * jnp.tanh(h)
    if keep is not None:
        y = y * keep
    out[f, r] = y.astype(BF16)


def build_taps(kernel, mid, side):
    zero = jnp.zeros((128, 128), BF16)
    tap = lambda a, i, j: kernel[a, (3 * i + j) * 128 : (3 * i + j + 1) * 128]
    for f in range(4):
        for i in range(3):
            at = pl.ds((3 * f + i) * 128, 128)
            mid[at, :128] = tap(f, i, 1) if f < 3 else zero
            mid[at, 128:] = tap(f - 1, i, 1) if f > 0 else zero
            if f < 3:
                side[at, :128] = tap(f, i, 0)
                side[at, 128:] = tap(f, i, 2)


def conv_pair(acts, mid, side, first, at, rows, put):
    pieces = [[acts[first + f, pl.ds(at + i, rows)].reshape(rows * 128, 128) for i in range(3)] for f in range(4)]
    dot = lambda blocks, taps: jnp.dot(jnp.concatenate(blocks, axis=-1), taps[...], preferred_element_type=F32)
    centre = dot(sum(pieces, []), mid)
    col = lax.broadcasted_iota(jnp.int32, (128, 128), 0)
    for o in range(2):
        sides = dot(sum(pieces[o : o + 3], []), side)
        for r in range(rows):
            here = slice(r * 128, (r + 1) * 128)
            left = jnp.where(col == 0, 0.0, pltpu.roll(sides[here, :128], 1, 0))
            right = jnp.where(col == 127, 0.0, pltpu.roll(sides[here, 128:], 127, 0))
            put(o, at + r, centre[here, o * 128 : (o + 1) * 128] + left + right)


def stats_kernel(x_hbm, *refs):
    small, (x_ref, pay_ref, z_ref, in_ref, far_ref, small_ref, sems) = refs[:6], refs[6:]
    frames, per = x_ref.shape[:2]
    copies = [pltpu.make_async_copy(x_hbm.at[f], x_ref.at[f], sems.at[f]) for f in range(frames)]
    copies += [pltpu.make_async_copy(v, small_ref.at[i], sems.at[frames + i]) for i, v in enumerate(small)]
    for copy in copies:
        copy.start()
    odd = (lax.axis_index("space") & 1) == 1
    cells = float(per * 128 * MEMBERS)
    load = lambda i: x_ref[i // per, i % per].astype(F32)
    for f in range(frames):
        copies[f].wait()
        if f == 0:
            mean, spread = local_stats(load, per, cells)
        for r in range(2):
            low, high = x_ref[f, r], x_ref[f, per - 2 + r]
            in_ref[f, r] = jnp.where(odd, low, high)
            far_ref[f, r] = jnp.where(odd, high, low)
    z_ref[...] = x_ref[2:]
    sums = shifted_sums(lambda i: load(per + i), (frames - 1) * per, mean)
    mean, spread = joined(mean, spread, cells, *sums, (frames - 1) * cells)
    pay_ref[...] = jnp.broadcast_to(payload(mean, spread)[:1], pay_ref.shape)
    for copy in copies[frames:]:
        copy.wait()


def pack_kernel(z_ref, near_ref, far_ref):
    per = z_ref.shape[1]
    odd = lax.axis_index("space") & 1
    for f in range(2):
        near_ref[f] = z_ref[f, pl.ds((1 - odd) * (per - 2), 2)]
        far_ref[f] = z_ref[f, pl.ds(odd * (per - 2), 2)]


def norm_constants(got_ref, small_ref, at, cells):
    mean, scale = whole_stats(got_ref, cells)
    gain, shift, bias = (small_ref[at + i : at + i + 1] for i in range(3))
    return mean[:1], scale[:1] * gain * 0.5, shift * 0.5, bias


def edges(strips):
    space = lax.axis_index("space")
    return jnp.where(space == 0, 0.0, 1.0), jnp.where(space == strips - 1, 0.0, 1.0)


def first_kernel(early, cells, strips, *refs):
    if early:
        kernel, consts_ref, small_ref, x_ref, in_ref, far_ref, z_ref, z_in_ref, z_far_ref, inner_ref, pay_ref, acts, mid, side = refs
        mean, slope, half, late, spread = (consts_ref[i : i + 1] for i in range(5))
        bias = small_ref[2:3]
    else:
        kernel_hbm, got_ref, small_ref, x_ref, in_ref, far_ref, inner_ref, send_ref, consts_ref, kernel, acts, mid, side, sem = refs
        fetch = pltpu.make_async_copy(kernel_hbm, kernel, sem)
        fetch.start()
        mean, slope, half, bias = norm_constants(got_ref, small_ref, 0, cells)
    top, bottom = edges(strips)
    odd = (lax.axis_index("space") & 1) == 1
    start = lax.axis_index("tm") == 0

    def act(own, near, far, f, r):
        if 2 <= r < 10:
            x, keep = own(r - 2), None
        else:
            high = r >= 10
            i = r - 10 if high else r
            a, b = near(i), far(i)
            x, keep = (jnp.where(odd, b, a), bottom) if high else (jnp.where(odd, a, b), top)
        put_act(x.astype(F32) - mean, slope, half, keep, acts, f, r)

    def of(ref, f):
        return lambda r: ref[f, r]

    def carried(ref, z, f):
        return lambda r: jnp.where(start, ref[0, r], z[f, r])

    def put(o, r, value):
        inner_ref[o, r] = value + bias

    done = 0
    for at, rows in (((0, 6), (6, 4)) if early else ((0, 5), (5, 5))):
        for r in range(done, at + rows + 2):
            for f in range(2):
                if early:
                    act(carried(x_ref, z_ref, f), carried(in_ref, z_in_ref, f), carried(far_ref, z_far_ref, f), f, r)
                    act(of(x_ref, f), of(in_ref, f), of(far_ref, f), 2 + f, r)
                else:
                    act(of(x_ref, 2 * f), of(in_ref, 2 * f), of(far_ref, 2 * f), 2 * f, r)
                    act(of(x_ref, 2 * f + 1), of(in_ref, 2 * f + 1), of(far_ref, 2 * f + 1), 2 * f + 1, r)
        done = at + rows + 2
        if at == 0:
            if not early:
                fetch.wait()
            build_taps(kernel, mid, side)
        conv_pair(acts, mid, side, 0, at, rows, put)
    own = lambda i: inner_ref[i // 8, 1 + i % 8]
    if early:
        m, spread = joined(late, spread, cells / 2, *shifted_sums(own, 16, late), cells / 2)
        m, spread, late = (jnp.broadcast_to(v[:1], (8, 128)) for v in (m, spread, late))
        pay_ref[...] = jnp.broadcast_to(payload(m, spread, late)[:1], pay_ref.shape)
    else:
        late, spread = local_stats(own, 16, cells / 2)
        for o in range(2):
            send_ref[o] = (inner_ref[o] - late[:1]).astype(BF16)
        for i, v in enumerate((mean, slope, half, late, spread)):
            consts_ref[i : i + 1] = v[:1]


def second_kernel(cells, strips, kernel_ref, got_ref, small_ref, feat_ref, b_ref, a_ref, z_ref, out_hbm, acts, mid, side, out, sems):
    mean, slope, half, bias = norm_constants(got_ref, small_ref, 3, cells)
    top, bottom = edges(strips)
    tm = lax.axis_index("tm")
    start = tm == 0
    sender = got_ref[pl.ds(jnp.maximum(tm - 1, 0) * strips + lax.axis_index("space"), 1)]
    base = mean - pick(jnp.broadcast_to(sender, (8, 128)), 2)[:1]

    def act(off, f, r):
        put_act(off, slope, half, {0: top, 9: bottom}.get(r), acts, f, r)

    copies = []

    def conv(pair, at, rows):
        def put(o, r, value):
            f = 2 * pair + o
            out[f, r] = feat_ref[f, r].astype(F32) + (value + bias)

        conv_pair(acts, mid, side, 2 * pair, at, rows, put)
        for o in range(2):
            f = 2 * pair + o
            here = (f, pl.ds(at, rows))
            copies.append(pltpu.make_async_copy(out.at[here], out_hbm.at[here], sems.at[len(copies)]))
            copies[-1].start()

    build_taps(kernel_ref, mid, side)
    for pair, chunks in ((1, ((0, 4), (4, 4))), (0, ((0, 5), (5, 3)))):
        done = 0
        for at, rows in chunks:
            for r in range(done, at + rows + 2):
                for f in range(4 if pair else 2):
                    if pair:
                        act((b_ref if f < 2 else a_ref)[f % 2, r] - mean, 2 + f, r)
                    else:
                        act(jnp.where(start, b_ref[0, r] - mean, z_ref[f, r].astype(F32) - base), f, r)
            done = at + rows + 2
            conv(pair, at, rows)
    for copy in copies:
        copy.wait()


VMEM = pl.BlockSpec(memory_space=pltpu.VMEM)
HBM = pl.BlockSpec(memory_space=pltpu.MemorySpace.HBM)
PARAMS = pltpu.CompilerParams(vmem_limit_bytes=32 * 1024 * 1024)
DMA = pltpu.SemaphoreType.DMA


def scratch(frames, rows):
    return [
        pltpu.VMEM((frames, rows, 128, 128), BF16),
        pltpu.VMEM((12 * 128, 256), BF16),
        pltpu.VMEM((9 * 128, 256), BF16),
    ]


def cost(pairs, rows):
    positions = pairs * rows * 128
    return pl.CostEstimate(
        flops=2 * positions * 36 * 128 * 256, bytes_accessed=4 << 20, transcendentals=2 * positions * 128
    )


def in_hbm(v):
    return pltpu.with_memory_space_constraint(v, pltpu.MemorySpace.HBM)


def shape(dims, dtype):
    return jax.ShapeDtypeStruct(dims, dtype)


def shards(features, gain_one, shift_one, kernel_one, bias_one, gain_two, shift_two, kernel_two, bias_two):
    slabs = lax.axis_size("tm")
    strips = lax.axis_size("space")
    devices = slabs * strips
    cells = float(4 * 8 * 128 * MEMBERS)
    swap_in = [(i, i ^ 1) for i in range(strips)]
    swap_far = [(i, (i + 1) % strips) for i in range(1, strips, 2)] + [((i + 1) % strips, i) for i in range(1, strips, 2)]
    later = [(i, (i + 1) % slabs) for i in range(slabs)]
    taps_one = kernel_one.reshape(3, 9 * 128, 128)
    taps_two = kernel_two.reshape(3, 9 * 128, 128)

    taps_one = in_hbm(taps_one)
    x, pay, z_send, in_send, far_send, small = pl.pallas_call(
        stats_kernel,
        out_shape=[
            shape((4, 8, 128, 128), BF16), shape((devices, 128), F32), shape((2, 8, 128, 128), BF16),
            shape((4, 2, 128, 128), BF16), shape((4, 2, 128, 128), BF16), shape((6, 128), F32),
        ],
        in_specs=[HBM] * 7, out_specs=[VMEM] * 6,
        scratch_shapes=[DMA((10,))], compiler_params=PARAMS,
        cost_estimate=pl.CostEstimate(flops=1 << 22, bytes_accessed=1 << 20, transcendentals=0), name="stats",
    )(*map(in_hbm, (features, gain_one, shift_one, bias_one, gain_two, shift_two, bias_two)))
    z_one = lax.ppermute(z_send, "tm", later)
    near = lax.ppermute(in_send, "space", swap_in)
    far = lax.ppermute(far_send, "space", swap_far)
    got = lax.all_to_all(pay, BOTH, 0, 0)
    near_send, far_send = pl.pallas_call(
        pack_kernel, out_shape=[shape((2, 2, 128, 128), BF16)] * 2, in_specs=[VMEM], out_specs=[VMEM] * 2, compiler_params=PARAMS,
        cost_estimate=pl.CostEstimate(flops=0, bytes_accessed=1 << 19, transcendentals=0), name="pack",
    )(z_one)
    z_near = lax.ppermute(near_send, "space", swap_in)
    z_far = lax.ppermute(far_send, "space", swap_far)
    inner_a, send, consts, kernel = pl.pallas_call(
        functools.partial(first_kernel, False, cells, strips),
        out_shape=[shape((2, 10, 128, 128), F32), shape((2, 10, 128, 128), BF16), shape((8, 128), F32), shape((3, 9 * 128, 128), BF16)],
        in_specs=[HBM] + [VMEM] * 5, out_specs=[VMEM] * 4, scratch_shapes=scratch(4, 12) + [DMA],
        compiler_params=PARAMS, cost_estimate=cost(1, 10), name="first_late",
    )(taps_one, got, small, x, near, far)
    z_two = lax.ppermute(send, "tm", later)
    inner_b, pay = pl.pallas_call(
        functools.partial(first_kernel, True, cells, strips),
        out_shape=[shape((2, 10, 128, 128), F32), shape((devices, 128), F32)],
        in_specs=[VMEM] * 9, out_specs=[VMEM] * 2, scratch_shapes=scratch(4, 12),
        compiler_params=PARAMS, cost_estimate=cost(1, 10), name="first_early",
    )(kernel, consts, small, x, near, far, z_one, z_near, z_far)
    got = lax.all_to_all(pay, BOTH, 0, 0)
    return pl.pallas_call(
        functools.partial(second_kernel, cells, strips),
        out_shape=shape((4, 8, 128, 128), F32),
        in_specs=[VMEM] * 7, out_specs=HBM,
        scratch_shapes=scratch(6, 10) + [pltpu.VMEM((4, 8, 128, 128), F32), DMA((8,))],
        compiler_params=PARAMS, cost_estimate=cost(2, 8), name="second",
    )(taps_two, got, small, x, inner_b, inner_a, z_two)


def solution(mesh):
    placed = (P("tm", "space", None, None), P(), P(), P(), P(), P(), P(), P(), P())
    return jax.shard_map(
        shards, mesh=mesh, in_specs=placed, out_specs=P("tm", "space", None, None), check_vma=False
    )
```

```python
import functools

import jax
import jax.numpy as jnp
from jax import lax
from jax.experimental import pallas as pl
from jax.experimental.pallas import tpu as pltpu
from jax.sharding import PartitionSpec as P

EPS = 1e-06
MEMBERS = 4
BOTH = ("tm", "space")
F32 = jnp.float32
BF16 = jnp.bfloat16


def lane_of(shape):
    return lax.broadcasted_iota(jnp.int32, shape, len(shape) - 1)


def group_sum(v):
    lane = lane_of(v.shape)
    width = v.shape[-1]
    axis = v.ndim - 1
    v = v + jnp.where((lane & 1) == 1, pltpu.roll(v, 1, axis), pltpu.roll(v, width - 1, axis))
    return v + jnp.where((lane & 2) == 2, pltpu.roll(v, 2, axis), pltpu.roll(v, width - 2, axis))


def column_sum(v):
    return jnp.broadcast_to(jnp.sum(v, axis=0, keepdims=True), (8, v.shape[1]))


def add_up(blocks):
    total = next(blocks)
    for block in blocks:
        total = total + block
    return total


def local_stats(load, rows, cells, total=None):
    if total is None:
        total = add_up(load(i) for i in range(rows))
    mean = group_sum(column_sum(total)) / cells

    def spread(i):
        d = load(i) - mean[:1]
        return d * d

    return mean, group_sum(column_sum(add_up(spread(i) for i in range(rows))))


def shifted_sums(load, rows, shift):
    first = second = None
    for i in range(rows):
        d = load(i) - shift[:1]
        first = d if i == 0 else first + d
        second = d * d if i == 0 else second + d * d
    return group_sum(column_sum(first)), group_sum(column_sum(second))


def joined(mean, spread, cells, first, second, more):
    whole = cells + more
    return mean + first / whole, spread + second - first * first / whole


def payload(*entries):
    place = lane_of(entries[0].shape) & 3
    out = jnp.zeros_like(entries[0])
    for i, entry in enumerate(entries):
        out = jnp.where(place == i, entry, out)
    return out


def pick(rows, place):
    return group_sum(jnp.where((lane_of(rows.shape) & 3) == place, rows, 0.0))


def whole_stats(got_ref, cells):
    got = got_ref[...]
    devices = got.shape[0]
    place = lane_of(got.shape) & 3
    off = got - got[:1]
    sums = jnp.where(place == 0, off, jnp.where(place == 1, got, 0.0))
    sums = column_sum(sums)
    squares = group_sum(column_sum(jnp.where(place == 0, off * off, 0.0)))
    here = lane_of(sums.shape) & 3
    shift = group_sum(jnp.where(here == 0, sums, 0.0)) / devices
    spread = group_sum(jnp.where(here == 1, sums, 0.0))
    first = group_sum(jnp.where(here == 0, jnp.broadcast_to(got[:1], sums.shape), 0.0))
    var = spread / (cells * devices) + (squares / devices - shift * shift)
    return first + shift, lax.rsqrt(var + EPS)


def put_act(off, slope, half_shift, keep, out, f, r):
    h = off * slope + half_shift
    y = h + h * jnp.tanh(h)
    if keep is not None:
        y = y * keep
    out[f, r] = y.astype(BF16)


def build_taps(kernel, mid, side):
    zero = jnp.zeros((128, 128), BF16)
    tap = lambda a, i, j: kernel[a, (3 * i + j) * 128 : (3 * i + j + 1) * 128]
    for f in range(4):
        for i in range(3):
            at = pl.ds((3 * f + i) * 128, 128)
            mid[at, :128] = tap(f, i, 1) if f < 3 else zero
            mid[at, 128:] = tap(f - 1, i, 1) if f > 0 else zero
            if f < 3:
                side[at, :128] = tap(f, i, 0)
                side[at, 128:] = tap(f, i, 2)


def conv_pair(acts, mid, side, first, at, rows, put):
    pieces = [[acts[first + f, pl.ds(at + i, rows)].reshape(rows * 128, 128) for i in range(3)] for f in range(4)]
    dot = lambda blocks, taps: jnp.dot(jnp.concatenate(blocks, axis=-1), taps[...], preferred_element_type=F32)
    centre = dot(sum(pieces, []), mid)
    col = lax.broadcasted_iota(jnp.int32, (128, 128), 0)
    for o in range(2):
        sides = dot(sum(pieces[o : o + 3], []), side)
        for r in range(rows):
            here = slice(r * 128, (r + 1) * 128)
            left = jnp.where(col == 0, 0.0, pltpu.roll(sides[here, :128], 1, 0))
            right = jnp.where(col == 127, 0.0, pltpu.roll(sides[here, 128:], 127, 0))
            put(o, at + r, centre[here, o * 128 : (o + 1) * 128] + left + right)


def stats_kernel(x_hbm, *refs):
    small, (x_ref, pay_ref, z_ref, in_ref, far_ref, small_ref, sems) = refs[:6], refs[6:]
    frames, per = x_ref.shape[:2]
    copies = [pltpu.make_async_copy(x_hbm.at[f], x_ref.at[f], sems.at[f]) for f in range(frames)]
    copies += [pltpu.make_async_copy(v, small_ref.at[i], sems.at[frames + i]) for i, v in enumerate(small)]
    for copy in copies:
        copy.start()
    odd = (lax.axis_index("space") & 1) == 1
    cells = float(per * 128 * MEMBERS)
    load = lambda i: x_ref[i // per, i % per].astype(F32)
    for f in range(frames):
        copies[f].wait()
        if f == 0:
            mean, spread = local_stats(load, per, cells)
        for r in range(2):
            low, high = x_ref[f, r], x_ref[f, per - 2 + r]
            in_ref[f, r] = jnp.where(odd, low, high)
            far_ref[f, r] = jnp.where(odd, high, low)
    z_ref[...] = x_ref[2:]
    sums = shifted_sums(lambda i: load(per + i), (frames - 1) * per, mean)
    mean, spread = joined(mean, spread, cells, *sums, (frames - 1) * cells)
    pay_ref[...] = jnp.broadcast_to(payload(mean, spread)[:1], pay_ref.shape)
    for copy in copies[frames:]:
        copy.wait()


def pack_kernel(kernel_hbm, z_ref, near_ref, far_ref, kernel_ref, sem):
    fetch = pltpu.make_async_copy(kernel_hbm, kernel_ref, sem)
    fetch.start()
    per = z_ref.shape[1]
    odd = lax.axis_index("space") & 1
    for f in range(2):
        near_ref[f] = z_ref[f, pl.ds((1 - odd) * (per - 2), 2)]
        far_ref[f] = z_ref[f, pl.ds(odd * (per - 2), 2)]
    fetch.wait()


def norm_constants(got_ref, small_ref, at, cells):
    mean, scale = whole_stats(got_ref, cells)
    gain, shift, bias = (small_ref[at + i : at + i + 1] for i in range(3))
    return mean[:1], scale[:1] * gain * 0.5, shift * 0.5, bias


def edges(strips):
    space = lax.axis_index("space")
    return jnp.where(space == 0, 0.0, 1.0), jnp.where(space == strips - 1, 0.0, 1.0)


def first_kernel(early, cells, strips, *refs):
    if early:
        kernel, consts_ref, small_ref, x_ref, in_ref, far_ref, z_ref, z_in_ref, z_far_ref, inner_ref, pay_ref, acts, mid, side = refs
        mean, slope, half, late, spread = (consts_ref[i : i + 1] for i in range(5))
        bias = small_ref[2:3]
    else:
        kernel, got_ref, small_ref, x_ref, in_ref, far_ref, inner_ref, send_ref, consts_ref, acts, mid, side = refs
        mean, slope, half, bias = norm_constants(got_ref, small_ref, 0, cells)
    top, bottom = edges(strips)
    odd = (lax.axis_index("space") & 1) == 1
    start = lax.axis_index("tm") == 0

    def act(own, near, far, f, r):
        if 2 <= r < 10:
            x, keep = own(r - 2), None
        else:
            high = r >= 10
            i = r - 10 if high else r
            a, b = near(i), far(i)
            x, keep = (jnp.where(odd, b, a), bottom) if high else (jnp.where(odd, a, b), top)
        put_act(x.astype(F32) - mean, slope, half, keep, acts, f, r)

    def of(ref, f):
        return lambda r: ref[f, r]

    def carried(ref, z, f):
        return lambda r: jnp.where(start, ref[0, r], z[f, r])

    def put(o, r, value):
        inner_ref[o, r] = value + bias

    done = 0
    for at, rows in (((0, 6), (6, 4)) if early else ((0, 5), (5, 5))):
        for r in range(done, at + rows + 2):
            for f in range(2):
                if early:
                    act(carried(x_ref, z_ref, f), carried(in_ref, z_in_ref, f), carried(far_ref, z_far_ref, f), f, r)
                    act(of(x_ref, f), of(in_ref, f), of(far_ref, f), 2 + f, r)
                else:
                    act(of(x_ref, 2 * f), of(in_ref, 2 * f), of(far_ref, 2 * f), 2 * f, r)
                    act(of(x_ref, 2 * f + 1), of(in_ref, 2 * f + 1), of(far_ref, 2 * f + 1), 2 * f + 1, r)
        done = at + rows + 2
        if at == 0:
            build_taps(kernel, mid, side)
        conv_pair(acts, mid, side, 0, at, rows, put)
    own = lambda i: inner_ref[i // 8, 1 + i % 8]
    if early:
        m, spread = joined(late, spread, cells / 2, *shifted_sums(own, 16, late), cells / 2)
        m, spread, late = (jnp.broadcast_to(v[:1], (8, 128)) for v in (m, spread, late))
        pay_ref[...] = jnp.broadcast_to(payload(m, spread, late)[:1], pay_ref.shape)
    else:
        late, spread = local_stats(own, 16, cells / 2)
        for o in range(2):
            send_ref[o] = (inner_ref[o] - late[:1]).astype(BF16)
        for i, v in enumerate((mean, slope, half, late, spread)):
            consts_ref[i : i + 1] = v[:1]


def second_kernel(cells, strips, kernel_ref, got_ref, small_ref, feat_ref, b_ref, a_ref, z_ref, out_hbm, acts, mid, side, out, sems):
    mean, slope, half, bias = norm_constants(got_ref, small_ref, 3, cells)
    top, bottom = edges(strips)
    tm = lax.axis_index("tm")
    start = tm == 0
    sender = got_ref[pl.ds(jnp.maximum(tm - 1, 0) * strips + lax.axis_index("space"), 1)]
    base = mean - pick(jnp.broadcast_to(sender, (8, 128)), 2)[:1]

    def act(off, f, r):
        put_act(off, slope, half, {0: top, 9: bottom}.get(r), acts, f, r)

    copies = []

    def conv(pair, at, rows):
        def put(o, r, value):
            f = 2 * pair + o
            out[f, r] = feat_ref[f, r].astype(F32) + (value + bias)

        conv_pair(acts, mid, side, 2 * pair, at, rows, put)
        for o in range(2):
            f = 2 * pair + o
            here = (f, pl.ds(at, rows))
            copies.append(pltpu.make_async_copy(out.at[here], out_hbm.at[here], sems.at[len(copies)]))
            copies[-1].start()

    build_taps(kernel_ref, mid, side)
    for pair, chunks in ((1, ((0, 4), (4, 4))), (0, ((0, 5), (5, 3)))):
        done = 0
        for at, rows in chunks:
            for r in range(done, at + rows + 2):
                for f in range(4 if pair else 2):
                    if pair:
                        act((b_ref if f < 2 else a_ref)[f % 2, r] - mean, 2 + f, r)
                    else:
                        act(jnp.where(start, b_ref[0, r] - mean, z_ref[f, r].astype(F32) - base), f, r)
            done = at + rows + 2
            conv(pair, at, rows)
    for copy in copies:
        copy.wait()


VMEM = pl.BlockSpec(memory_space=pltpu.VMEM)
HBM = pl.BlockSpec(memory_space=pltpu.MemorySpace.HBM)
PARAMS = pltpu.CompilerParams(vmem_limit_bytes=32 * 1024 * 1024)
DMA = pltpu.SemaphoreType.DMA


def scratch(frames, rows):
    return [
        pltpu.VMEM((frames, rows, 128, 128), BF16),
        pltpu.VMEM((12 * 128, 256), BF16),
        pltpu.VMEM((9 * 128, 256), BF16),
    ]


def cost(pairs, rows):
    positions = pairs * rows * 128
    return pl.CostEstimate(
        flops=2 * positions * 36 * 128 * 256, bytes_accessed=4 << 20, transcendentals=2 * positions * 128
    )


def in_hbm(v):
    return pltpu.with_memory_space_constraint(v, pltpu.MemorySpace.HBM)


def shape(dims, dtype):
    return jax.ShapeDtypeStruct(dims, dtype)


def shards(features, gain_one, shift_one, kernel_one, bias_one, gain_two, shift_two, kernel_two, bias_two):
    slabs = lax.axis_size("tm")
    strips = lax.axis_size("space")
    devices = slabs * strips
    cells = float(4 * 8 * 128 * MEMBERS)
    swap_in = [(i, i ^ 1) for i in range(strips)]
    swap_far = [(i, (i + 1) % strips) for i in range(1, strips, 2)] + [((i + 1) % strips, i) for i in range(1, strips, 2)]
    later = [(i, (i + 1) % slabs) for i in range(slabs)]
    taps_one = kernel_one.reshape(3, 9 * 128, 128)
    taps_two = kernel_two.reshape(3, 9 * 128, 128)

    taps_one = in_hbm(taps_one)
    x, pay, z_send, in_send, far_send, small = pl.pallas_call(
        stats_kernel,
        out_shape=[
            shape((4, 8, 128, 128), BF16), shape((devices, 128), F32), shape((2, 8, 128, 128), BF16),
            pltpu.HBM((4, 2, 128, 128), BF16), pltpu.HBM((4, 2, 128, 128), BF16), shape((6, 128), F32),
        ],
        in_specs=[HBM] * 7, out_specs=[VMEM] * 6,
        scratch_shapes=[DMA((10,))], compiler_params=PARAMS,
        cost_estimate=pl.CostEstimate(flops=1 << 22, bytes_accessed=1 << 20, transcendentals=0), name="stats",
    )(*map(in_hbm, (features, gain_one, shift_one, bias_one, gain_two, shift_two, bias_two)))
    z_one = lax.ppermute(z_send, "tm", later)
    near = lax.ppermute(in_send, "space", swap_in)
    far = lax.ppermute(far_send, "space", swap_far)
    got = lax.all_to_all(pay, BOTH, 0, 0)
    near_send, far_send, taps_one = pl.pallas_call(
        pack_kernel, out_shape=[pltpu.HBM((2, 2, 128, 128), BF16)] * 2 + [shape((3, 9 * 128, 128), BF16)],
        in_specs=[HBM, VMEM], out_specs=[VMEM] * 3, scratch_shapes=[DMA], compiler_params=PARAMS,
        cost_estimate=pl.CostEstimate(flops=0, bytes_accessed=1 << 19, transcendentals=0), name="pack",
    )(taps_one, z_one)
    z_near = lax.ppermute(near_send, "space", swap_in)
    z_far = lax.ppermute(far_send, "space", swap_far)
    inner_a, send, consts = pl.pallas_call(
        functools.partial(first_kernel, False, cells, strips),
        out_shape=[shape((2, 10, 128, 128), F32), shape((2, 10, 128, 128), BF16), shape((8, 128), F32)],
        in_specs=[VMEM] * 6, out_specs=[VMEM] * 3, scratch_shapes=scratch(4, 12),
        compiler_params=PARAMS, cost_estimate=cost(1, 10), name="first_late",
    )(taps_one, got, small, x, near, far)
    z_two = lax.ppermute(send, "tm", later)
    inner_b, pay = pl.pallas_call(
        functools.partial(first_kernel, True, cells, strips),
        out_shape=[shape((2, 10, 128, 128), F32), shape((devices, 128), F32)],
        in_specs=[VMEM] * 9, out_specs=[VMEM] * 2, scratch_shapes=scratch(4, 12),
        compiler_params=PARAMS, cost_estimate=cost(1, 10), name="first_early",
    )(taps_one, consts, small, x, near, far, z_one, z_near, z_far)
    got = lax.all_to_all(pay, BOTH, 0, 0)
    return pl.pallas_call(
        functools.partial(second_kernel, cells, strips),
        out_shape=shape((4, 8, 128, 128), F32),
        in_specs=[VMEM] * 7, out_specs=HBM,
        scratch_shapes=scratch(6, 10) + [pltpu.VMEM((4, 8, 128, 128), F32), DMA((8,))],
        compiler_params=PARAMS, cost_estimate=cost(2, 8), name="second",
    )(taps_two, got, small, x, inner_b, inner_a, z_two)


def solution(mesh):
    placed = (P("tm", "space", None, None), P(), P(), P(), P(), P(), P(), P(), P())
    return jax.shard_map(
        shards, mesh=mesh, in_specs=placed, out_specs=P("tm", "space", None, None), check_vma=False
    )
```

```python
import functools

import jax
import jax.numpy as jnp
from jax import lax
from jax.experimental import pallas as pl
from jax.experimental.pallas import tpu as pltpu
from jax.sharding import PartitionSpec as P

EPS = 1e-06
MEMBERS = 4
BOTH = ("tm", "space")
F32 = jnp.float32
BF16 = jnp.bfloat16


def lane_of(shape):
    return lax.broadcasted_iota(jnp.int32, shape, len(shape) - 1)


def group_sum(v):
    lane = lane_of(v.shape)
    width = v.shape[-1]
    axis = v.ndim - 1
    v = v + jnp.where((lane & 1) == 1, pltpu.roll(v, 1, axis), pltpu.roll(v, width - 1, axis))
    return v + jnp.where((lane & 2) == 2, pltpu.roll(v, 2, axis), pltpu.roll(v, width - 2, axis))


def column_sum(v):
    return jnp.broadcast_to(jnp.sum(v, axis=0, keepdims=True), (8, v.shape[1]))


def add_up(blocks):
    total = next(blocks)
    for block in blocks:
        total = total + block
    return total


def local_stats(load, rows, cells, total=None):
    if total is None:
        total = add_up(load(i) for i in range(rows))
    mean = group_sum(column_sum(total)) / cells

    def spread(i):
        d = load(i) - mean[:1]
        return d * d

    return mean, group_sum(column_sum(add_up(spread(i) for i in range(rows))))


def shifted_sums(load, rows, shift):
    first = second = None
    for i in range(rows):
        d = load(i) - shift[:1]
        first = d if i == 0 else first + d
        second = d * d if i == 0 else second + d * d
    return group_sum(column_sum(first)), group_sum(column_sum(second))


def joined(mean, spread, cells, first, second, more):
    whole = cells + more
    return mean + first / whole, spread + second - first * first / whole


def payload(*entries):
    place = lane_of(entries[0].shape) & 3
    out = jnp.zeros_like(entries[0])
    for i, entry in enumerate(entries):
        out = jnp.where(place == i, entry, out)
    return out


def pick(rows, place):
    return group_sum(jnp.where((lane_of(rows.shape) & 3) == place, rows, 0.0))


def whole_stats(got_ref, cells):
    got = got_ref[...]
    devices = got.shape[0]
    place = lane_of(got.shape) & 3
    off = got - got[:1]
    sums = jnp.where(place == 0, off, jnp.where(place == 1, got, 0.0))
    sums = column_sum(sums)
    squares = group_sum(column_sum(jnp.where(place == 0, off * off, 0.0)))
    here = lane_of(sums.shape) & 3
    shift = group_sum(jnp.where(here == 0, sums, 0.0)) / devices
    spread = group_sum(jnp.where(here == 1, sums, 0.0))
    first = group_sum(jnp.where(here == 0, jnp.broadcast_to(got[:1], sums.shape), 0.0))
    var = spread / (cells * devices) + (squares / devices - shift * shift)
    return first + shift, lax.rsqrt(var + EPS)


def put_act(off, slope, half_shift, keep, out, f, r):
    h = off * slope + half_shift
    y = h + h * jnp.tanh(h)
    if keep is not None:
        y = y * keep
    out[f, r] = y.astype(BF16)


def build_taps(kernel, mid, side):
    zero = jnp.zeros((128, 128), BF16)
    tap = lambda a, i, j: kernel[a, (3 * i + j) * 128 : (3 * i + j + 1) * 128]
    for f in range(4):
        for i in range(3):
            at = pl.ds((3 * f + i) * 128, 128)
            mid[at, :128] = tap(f, i, 1) if f < 3 else zero
            mid[at, 128:] = tap(f - 1, i, 1) if f > 0 else zero
            if f < 3:
                side[at, :128] = tap(f, i, 0)
                side[at, 128:] = tap(f, i, 2)


def conv_pair(acts, mid, side, first, at, rows, put):
    pieces = [[acts[first + f, pl.ds(at + i, rows)].reshape(rows * 128, 128) for i in range(3)] for f in range(4)]
    dot = lambda blocks, taps: jnp.dot(jnp.concatenate(blocks, axis=-1), taps[...], preferred_element_type=F32)
    centre = dot(sum(pieces, []), mid)
    col = lax.broadcasted_iota(jnp.int32, (128, 128), 0)
    for o in range(2):
        sides = dot(sum(pieces[o : o + 3], []), side)
        for r in range(rows):
            here = slice(r * 128, (r + 1) * 128)
            left = jnp.where(col == 0, 0.0, pltpu.roll(sides[here, :128], 1, 0))
            right = jnp.where(col == 127, 0.0, pltpu.roll(sides[here, 128:], 127, 0))
            put(o, at + r, centre[here, o * 128 : (o + 1) * 128] + left + right)


def stats_kernel(x_hbm, *refs):
    small, (x_ref, pay_ref, z_ref, in_out, far_out, small_ref, in_ref, far_ref, sems, out_sems) = refs[:6], refs[6:]
    frames, per = x_ref.shape[:2]
    copies = [pltpu.make_async_copy(x_hbm.at[f], x_ref.at[f], sems.at[f]) for f in range(frames)]
    copies += [pltpu.make_async_copy(v, small_ref.at[i], sems.at[frames + i]) for i, v in enumerate(small)]
    for copy in copies:
        copy.start()
    odd = (lax.axis_index("space") & 1) == 1
    cells = float(per * 128 * MEMBERS)
    load = lambda i: x_ref[i // per, i % per].astype(F32)
    for f in range(frames):
        copies[f].wait()
        if f == 0:
            mean, spread = local_stats(load, per, cells)
        for r in range(2):
            low, high = x_ref[f, r], x_ref[f, per - 2 + r]
            in_ref[f, r] = jnp.where(odd, low, high)
            far_ref[f, r] = jnp.where(odd, high, low)
    leaving = [
        pltpu.make_async_copy(in_ref, in_out, out_sems.at[0]),
        pltpu.make_async_copy(far_ref, far_out, out_sems.at[1]),
    ]
    for copy in leaving:
        copy.start()
    z_ref[...] = x_ref[2:]
    sums = shifted_sums(lambda i: load(per + i), (frames - 1) * per, mean)
    mean, spread = joined(mean, spread, cells, *sums, (frames - 1) * cells)
    pay_ref[...] = jnp.broadcast_to(payload(mean, spread)[:1], pay_ref.shape)
    for copy in copies[frames:] + leaving:
        copy.wait()


def pack_kernel(kernel_hbm, z_ref, near_ref, far_ref, kernel_ref, sem):
    fetch = pltpu.make_async_copy(kernel_hbm, kernel_ref, sem)
    fetch.start()
    per = z_ref.shape[1]
    odd = lax.axis_index("space") & 1
    for f in range(2):
        near_ref[f] = z_ref[f, pl.ds((1 - odd) * (per - 2), 2)]
        far_ref[f] = z_ref[f, pl.ds(odd * (per - 2), 2)]
    fetch.wait()


def norm_constants(got_ref, small_ref, at, cells):
    mean, scale = whole_stats(got_ref, cells)
    gain, shift, bias = (small_ref[at + i : at + i + 1] for i in range(3))
    return mean[:1], scale[:1] * gain * 0.5, shift * 0.5, bias


def edges(strips):
    space = lax.axis_index("space")
    return jnp.where(space == 0, 0.0, 1.0), jnp.where(space == strips - 1, 0.0, 1.0)


def first_kernel(early, cells, strips, *refs):
    if early:
        mid, side, consts_ref, small_ref, x_ref, in_ref, far_ref, z_ref, z_in_ref, z_far_ref, inner_ref, pay_ref, acts = refs
        mean, slope, half, late, spread = (consts_ref[i : i + 1] for i in range(5))
        bias = small_ref[2:3]
    else:
        kernel, got_ref, small_ref, x_ref, in_ref, far_ref, inner_ref, send_ref, consts_ref, mid, side, acts = refs
        mean, slope, half, bias = norm_constants(got_ref, small_ref, 0, cells)
    top, bottom = edges(strips)
    odd = (lax.axis_index("space") & 1) == 1
    start = lax.axis_index("tm") == 0

    def act(own, near, far, f, r):
        if 2 <= r < 10:
            x, keep = own(r - 2), None
        else:
            high = r >= 10
            i = r - 10 if high else r
            a, b = near(i), far(i)
            x, keep = (jnp.where(odd, b, a), bottom) if high else (jnp.where(odd, a, b), top)
        put_act(x.astype(F32) - mean, slope, half, keep, acts, f, r)

    def of(ref, f):
        return lambda r: ref[f, r]

    def carried(ref, z, f):
        return lambda r: jnp.where(start, ref[0, r], z[f, r])

    def put(o, r, value):
        inner_ref[o, r] = value + bias

    done = 0
    for at, rows in ((0, 6), (6, 4)):
        for r in range(done, at + rows + 2):
            for f in range(2):
                if early:
                    act(carried(x_ref, z_ref, f), carried(in_ref, z_in_ref, f), carried(far_ref, z_far_ref, f), f, r)
                    act(of(x_ref, f), of(in_ref, f), of(far_ref, f), 2 + f, r)
                else:
                    act(of(x_ref, 2 * f), of(in_ref, 2 * f), of(far_ref, 2 * f), 2 * f, r)
                    act(of(x_ref, 2 * f + 1), of(in_ref, 2 * f + 1), of(far_ref, 2 * f + 1), 2 * f + 1, r)
        done = at + rows + 2
        if at == 0:
            if not early:
                build_taps(kernel, mid, side)
        conv_pair(acts, mid, side, 0, at, rows, put)
    own = lambda i: inner_ref[i // 8, 1 + i % 8]
    if early:
        m, spread = joined(late, spread, cells / 2, *shifted_sums(own, 16, late), cells / 2)
        m, spread, late = (jnp.broadcast_to(v[:1], (8, 128)) for v in (m, spread, late))
        pay_ref[...] = jnp.broadcast_to(payload(m, spread, late)[:1], pay_ref.shape)
    else:
        late, spread = local_stats(own, 16, cells / 2)
        for o in range(2):
            send_ref[o] = (inner_ref[o] - late[:1]).astype(BF16)
        for i, v in enumerate((mean, slope, half, late, spread)):
            consts_ref[i : i + 1] = v[:1]


def second_kernel(cells, strips, kernel_ref, got_ref, small_ref, feat_ref, b_ref, a_ref, z_ref, out_hbm, acts, mid, side, out, sems):
    mean, slope, half, bias = norm_constants(got_ref, small_ref, 3, cells)
    top, bottom = edges(strips)
    tm = lax.axis_index("tm")
    start = tm == 0
    sender = got_ref[pl.ds(jnp.maximum(tm - 1, 0) * strips + lax.axis_index("space"), 1)]
    base = mean - pick(jnp.broadcast_to(sender, (8, 128)), 2)[:1]

    def act(off, f, r):
        put_act(off, slope, half, {0: top, 9: bottom}.get(r), acts, f, r)

    copies = []

    def conv(pair, at, rows):
        def put(o, r, value):
            f = 2 * pair + o
            out[f, r] = feat_ref[f, r].astype(F32) + (value + bias)

        conv_pair(acts, mid, side, 2 * pair, at, rows, put)
        for o in range(2):
            f = 2 * pair + o
            here = (f, pl.ds(at, rows))
            copies.append(pltpu.make_async_copy(out.at[here], out_hbm.at[here], sems.at[len(copies)]))
            copies[-1].start()

    build_taps(kernel_ref, mid, side)
    for pair, chunks in ((1, ((0, 4), (4, 4))), (0, ((0, 5), (5, 3)))):
        done = 0
        for at, rows in chunks:
            for r in range(done, at + rows + 2):
                for f in range(4 if pair else 2):
                    if pair:
                        act((b_ref if f < 2 else a_ref)[f % 2, r] - mean, 2 + f, r)
                    else:
                        act(jnp.where(start, b_ref[0, r] - mean, z_ref[f, r].astype(F32) - base), f, r)
            done = at + rows + 2
            conv(pair, at, rows)
    for copy in copies:
        copy.wait()


VMEM = pl.BlockSpec(memory_space=pltpu.VMEM)
HBM = pl.BlockSpec(memory_space=pltpu.MemorySpace.HBM)
PARAMS = pltpu.CompilerParams(vmem_limit_bytes=32 * 1024 * 1024)
DMA = pltpu.SemaphoreType.DMA


def scratch(frames, rows):
    return [
        pltpu.VMEM((frames, rows, 128, 128), BF16),
        pltpu.VMEM((12 * 128, 256), BF16),
        pltpu.VMEM((9 * 128, 256), BF16),
    ]


def cost(pairs, rows):
    positions = pairs * rows * 128
    return pl.CostEstimate(
        flops=2 * positions * 36 * 128 * 256, bytes_accessed=4 << 20, transcendentals=2 * positions * 128
    )


def in_hbm(v):
    return pltpu.with_memory_space_constraint(v, pltpu.MemorySpace.HBM)


def shape(dims, dtype):
    return jax.ShapeDtypeStruct(dims, dtype)


def shards(features, gain_one, shift_one, kernel_one, bias_one, gain_two, shift_two, kernel_two, bias_two):
    slabs = lax.axis_size("tm")
    strips = lax.axis_size("space")
    devices = slabs * strips
    cells = float(4 * 8 * 128 * MEMBERS)
    swap_in = [(i, i ^ 1) for i in range(strips)]
    swap_far = [(i, (i + 1) % strips) for i in range(1, strips, 2)] + [((i + 1) % strips, i) for i in range(1, strips, 2)]
    later = [(i, (i + 1) % slabs) for i in range(slabs)]
    taps_one = kernel_one.reshape(3, 9 * 128, 128)
    taps_two = kernel_two.reshape(3, 9 * 128, 128)

    taps_one = in_hbm(taps_one)
    x, pay, z_send, in_send, far_send, small = pl.pallas_call(
        stats_kernel,
        out_shape=[
            shape((4, 8, 128, 128), BF16), shape((devices, 128), F32), shape((2, 8, 128, 128), BF16),
            pltpu.HBM((4, 2, 128, 128), BF16), pltpu.HBM((4, 2, 128, 128), BF16), shape((6, 128), F32),
        ],
        in_specs=[HBM] * 7, out_specs=[VMEM] * 3 + [HBM] * 2 + [VMEM],
        scratch_shapes=[pltpu.VMEM((4, 2, 128, 128), BF16)] * 2 + [DMA((10,)), DMA((2,))], compiler_params=PARAMS,
        cost_estimate=pl.CostEstimate(flops=1 << 22, bytes_accessed=1 << 20, transcendentals=0), name="stats",
    )(*map(in_hbm, (features, gain_one, shift_one, bias_one, gain_two, shift_two, bias_two)))
    z_one = lax.ppermute(z_send, "tm", later)
    near = lax.ppermute(in_send, "space", swap_in)
    far = lax.ppermute(far_send, "space", swap_far)
    got = lax.all_to_all(pay, BOTH, 0, 0)
    near_send, far_send, taps_one = pl.pallas_call(
        pack_kernel, out_shape=[pltpu.HBM((2, 2, 128, 128), BF16)] * 2 + [shape((3, 9 * 128, 128), BF16)],
        in_specs=[HBM, VMEM], out_specs=[VMEM] * 3, scratch_shapes=[DMA], compiler_params=PARAMS,
        cost_estimate=pl.CostEstimate(flops=0, bytes_accessed=1 << 19, transcendentals=0), name="pack",
    )(taps_one, z_one)
    z_near = lax.ppermute(near_send, "space", swap_in)
    z_far = lax.ppermute(far_send, "space", swap_far)
    inner_a, send, consts, mid, side = pl.pallas_call(
        functools.partial(first_kernel, False, cells, strips),
        out_shape=[shape((2, 10, 128, 128), F32), shape((2, 10, 128, 128), BF16), shape((8, 128), F32)]
        + [shape((n * 128, 256), BF16) for n in (12, 9)],
        in_specs=[VMEM] * 6, out_specs=[VMEM] * 5, scratch_shapes=scratch(4, 12)[:1],
        compiler_params=PARAMS, cost_estimate=cost(1, 10), name="first_late",
    )(taps_one, got, small, x, near, far)
    z_two = lax.ppermute(send, "tm", later)
    inner_b, pay = pl.pallas_call(
        functools.partial(first_kernel, True, cells, strips),
        out_shape=[shape((2, 10, 128, 128), F32), shape((devices, 128), F32)],
        in_specs=[VMEM] * 10, out_specs=[VMEM] * 2, scratch_shapes=scratch(4, 12)[:1],
        compiler_params=PARAMS, cost_estimate=cost(1, 10), name="first_early",
    )(mid, side, consts, small, x, near, far, z_one, z_near, z_far)
    got = lax.all_to_all(pay, BOTH, 0, 0)
    return pl.pallas_call(
        functools.partial(second_kernel, cells, strips),
        out_shape=shape((4, 8, 128, 128), F32),
        in_specs=[VMEM] * 7, out_specs=HBM,
        scratch_shapes=scratch(6, 10) + [pltpu.VMEM((4, 8, 128, 128), F32), DMA((8,))],
        compiler_params=PARAMS, cost_estimate=cost(2, 8), name="second",
    )(taps_two, got, small, x, inner_b, inner_a, z_two)


def solution(mesh):
    placed = (P("tm", "space", None, None), P(), P(), P(), P(), P(), P(), P(), P())
    return jax.shard_map(
        shards, mesh=mesh, in_specs=placed, out_specs=P("tm", "space", None, None), check_vma=False
    )
```

```python
import functools

import jax
import jax.numpy as jnp
from jax import lax
from jax.experimental import pallas as pl
from jax.experimental.pallas import tpu as pltpu
from jax.sharding import PartitionSpec as P

EPS = 1e-06
MEMBERS = 4
BOTH = ("tm", "space")
F32 = jnp.float32
BF16 = jnp.bfloat16


def lane_of(shape):
    return lax.broadcasted_iota(jnp.int32, shape, len(shape) - 1)


def group_sum(v):
    lane = lane_of(v.shape)
    width = v.shape[-1]
    axis = v.ndim - 1
    v = v + jnp.where((lane & 1) == 1, pltpu.roll(v, 1, axis), pltpu.roll(v, width - 1, axis))
    return v + jnp.where((lane & 2) == 2, pltpu.roll(v, 2, axis), pltpu.roll(v, width - 2, axis))


def column_sum(v):
    return jnp.broadcast_to(jnp.sum(v, axis=0, keepdims=True), (8, v.shape[1]))


def add_up(blocks):
    total = next(blocks)
    for block in blocks:
        total = total + block
    return total


def local_stats(load, rows, cells, total=None):
    if total is None:
        total = add_up(load(i) for i in range(rows))
    mean = group_sum(column_sum(total)) / cells

    def spread(i):
        d = load(i) - mean[:1]
        return d * d

    return mean, group_sum(column_sum(add_up(spread(i) for i in range(rows))))


def shifted_sums(load, rows, shift):
    first = second = None
    for i in range(rows):
        d = load(i) - shift[:1]
        first = d if i == 0 else first + d
        second = d * d if i == 0 else second + d * d
    return group_sum(column_sum(first)), group_sum(column_sum(second))


def joined(mean, spread, cells, first, second, more):
    whole = cells + more
    return mean + first / whole, spread + second - first * first / whole


def payload(*entries):
    place = lane_of(entries[0].shape) & 3
    out = jnp.zeros_like(entries[0])
    for i, entry in enumerate(entries):
        out = jnp.where(place == i, entry, out)
    return out


def pick(rows, place):
    return group_sum(jnp.where((lane_of(rows.shape) & 3) == place, rows, 0.0))


def whole_stats(got_ref, cells):
    got = got_ref[...]
    devices = got.shape[0]
    place = lane_of(got.shape) & 3
    off = got - got[:1]
    sums = jnp.where(place == 0, off, jnp.where(place == 1, got, 0.0))
    sums = column_sum(sums)
    squares = group_sum(column_sum(jnp.where(place == 0, off * off, 0.0)))
    here = lane_of(sums.shape) & 3
    shift = group_sum(jnp.where(here == 0, sums, 0.0)) / devices
    spread = group_sum(jnp.where(here == 1, sums, 0.0))
    first = group_sum(jnp.where(here == 0, jnp.broadcast_to(got[:1], sums.shape), 0.0))
    var = spread / (cells * devices) + (squares / devices - shift * shift)
    return first + shift, lax.rsqrt(var + EPS)


def put_act(off, slope, half_shift, keep, out, f, r):
    h = off * slope + half_shift
    y = h + h * jnp.tanh(h)
    if keep is not None:
        y = y * keep
    out[f, r] = y.astype(BF16)


def build_taps(kernel, mid, side):
    zero = jnp.zeros((128, 128), BF16)
    tap = lambda a, i, j: kernel[a, (3 * i + j) * 128 : (3 * i + j + 1) * 128]
    for f in range(4):
        for i in range(3):
            at = pl.ds((3 * f + i) * 128, 128)
            mid[at, :128] = tap(f, i, 1) if f < 3 else zero
            mid[at, 128:] = tap(f - 1, i, 1) if f > 0 else zero
            if f < 3:
                side[at, :128] = tap(f, i, 0)
                side[at, 128:] = tap(f, i, 2)


def conv_pair(acts, mid, side, first, at, rows, put):
    pieces = [[acts[first + f, pl.ds(at + i, rows)].reshape(rows * 128, 128) for i in range(3)] for f in range(4)]
    dot = lambda blocks, taps: jnp.dot(jnp.concatenate(blocks, axis=-1), taps[...], preferred_element_type=F32)
    centre = dot(sum(pieces, []), mid)
    col = lax.broadcasted_iota(jnp.int32, (128, 128), 0)
    for o in range(2):
        sides = dot(sum(pieces[o : o + 3], []), side)
        for r in range(rows):
            here = slice(r * 128, (r + 1) * 128)
            left = jnp.where(col == 0, 0.0, pltpu.roll(sides[here, :128], 1, 0))
            right = jnp.where(col == 127, 0.0, pltpu.roll(sides[here, 128:], 127, 0))
            put(o, at + r, centre[here, o * 128 : (o + 1) * 128] + left + right)


def stats_kernel(x_hbm, x_ref, pay_ref, z_ref, in_ref, far_ref, sems):
    frames, per = x_ref.shape[:2]
    copies = [pltpu.make_async_copy(x_hbm.at[f], x_ref.at[f], sems.at[f]) for f in range(frames)]
    for copy in copies:
        copy.start()
    odd = (lax.axis_index("space") & 1) == 1
    cells = float(per * 128 * MEMBERS)
    load = lambda i: x_ref[i // per, i % per].astype(F32)
    for f in range(frames):
        copies[f].wait()
        if f == 0:
            mean, spread = local_stats(load, per, cells)
        for r in range(2):
            low, high = x_ref[f, r], x_ref[f, per - 2 + r]
            in_ref[f, r] = jnp.where(odd, low, high)
            far_ref[f, r] = jnp.where(odd, high, low)
    z_ref[...] = x_ref[2:]
    sums = shifted_sums(lambda i: load(per + i), (frames - 1) * per, mean)
    mean, spread = joined(mean, spread, cells, *sums, (frames - 1) * cells)
    pay_ref[...] = jnp.broadcast_to(payload(mean, spread)[:1], pay_ref.shape)


def pack_kernel(kernel_hbm, *refs):
    small, (z_ref, near_ref, far_ref, kernel_ref, small_ref, sems) = refs[:6], refs[6:]
    fetch = [pltpu.make_async_copy(v, small_ref.at[i], sems.at[i]) for i, v in enumerate(small)]
    fetch.append(pltpu.make_async_copy(kernel_hbm, kernel_ref, sems.at[6]))
    for copy in fetch:
        copy.start()
    per = z_ref.shape[1]
    odd = lax.axis_index("space") & 1
    for f in range(2):
        near_ref[f] = z_ref[f, pl.ds((1 - odd) * (per - 2), 2)]
        far_ref[f] = z_ref[f, pl.ds(odd * (per - 2), 2)]
    for copy in fetch:
        copy.wait()


def norm_constants(got_ref, small_ref, at, cells):
    mean, scale = whole_stats(got_ref, cells)
    gain, shift, bias = (small_ref[at + i : at + i + 1] for i in range(3))
    return mean[:1], scale[:1] * gain * 0.5, shift * 0.5, bias


def edges(strips):
    space = lax.axis_index("space")
    return jnp.where(space == 0, 0.0, 1.0), jnp.where(space == strips - 1, 0.0, 1.0)


def first_kernel(early, cells, strips, *refs):
    if early:
        kernel, consts_ref, small_ref, x_ref, in_ref, far_ref, z_ref, z_in_ref, z_far_ref, inner_ref, pay_ref, acts, mid, side = refs
        mean, slope, half, late, spread = (consts_ref[i : i + 1] for i in range(5))
        bias = small_ref[2:3]
    else:
        kernel, got_ref, small_ref, x_ref, in_ref, far_ref, inner_ref, send_ref, consts_ref, acts, mid, side = refs
        mean, slope, half, bias = norm_constants(got_ref, small_ref, 0, cells)
    top, bottom = edges(strips)
    odd = (lax.axis_index("space") & 1) == 1
    start = lax.axis_index("tm") == 0

    def act(own, near, far, f, r):
        if 2 <= r < 10:
            x, keep = own(r - 2), None
        else:
            high = r >= 10
            i = r - 10 if high else r
            a, b = near(i), far(i)
            x, keep = (jnp.where(odd, b, a), bottom) if high else (jnp.where(odd, a, b), top)
        put_act(x.astype(F32) - mean, slope, half, keep, acts, f, r)

    def of(ref, f):
        return lambda r: ref[f, r]

    def carried(ref, z, f):
        return lambda r: jnp.where(start, ref[0, r], z[f, r])

    def put(o, r, value):
        inner_ref[o, r] = value + bias

    done = 0
    for at, rows in (((0, 6), (6, 4)) if early else ((0, 5), (5, 5))):
        for r in range(done, at + rows + 2):
            for f in range(2):
                if early:
                    act(carried(x_ref, z_ref, f), carried(in_ref, z_in_ref, f), carried(far_ref, z_far_ref, f), f, r)
                    act(of(x_ref, f), of(in_ref, f), of(far_ref, f), 2 + f, r)
                else:
                    act(of(x_ref, 2 * f), of(in_ref, 2 * f), of(far_ref, 2 * f), 2 * f, r)
                    act(of(x_ref, 2 * f + 1), of(in_ref, 2 * f + 1), of(far_ref, 2 * f + 1), 2 * f + 1, r)
        done = at + rows + 2
        if at == 0:
            build_taps(kernel, mid, side)
        conv_pair(acts, mid, side, 0, at, rows, put)
    own = lambda i: inner_ref[i // 8, 1 + i % 8]
    if early:
        m, spread = joined(late, spread, cells / 2, *shifted_sums(own, 16, late), cells / 2)
        m, spread, late = (jnp.broadcast_to(v[:1], (8, 128)) for v in (m, spread, late))
        pay_ref[...] = jnp.broadcast_to(payload(m, spread, late)[:1], pay_ref.shape)
    else:
        late, spread = local_stats(own, 16, cells / 2)
        for o in range(2):
            send_ref[o] = (inner_ref[o] - late[:1]).astype(BF16)
        for i, v in enumerate((mean, slope, half, late, spread)):
            consts_ref[i : i + 1] = v[:1]


def second_kernel(cells, strips, kernel_ref, got_ref, small_ref, feat_ref, b_ref, a_ref, z_ref, out_hbm, acts, mid, side, out, sems):
    mean, slope, half, bias = norm_constants(got_ref, small_ref, 3, cells)
    top, bottom = edges(strips)
    tm = lax.axis_index("tm")
    start = tm == 0
    sender = got_ref[pl.ds(jnp.maximum(tm - 1, 0) * strips + lax.axis_index("space"), 1)]
    base = mean - pick(jnp.broadcast_to(sender, (8, 128)), 2)[:1]

    def act(off, f, r):
        put_act(off, slope, half, {0: top, 9: bottom}.get(r), acts, f, r)

    copies = []

    def conv(pair, at, rows):
        def put(o, r, value):
            f = 2 * pair + o
            out[f, r] = feat_ref[f, r].astype(F32) + (value + bias)

        conv_pair(acts, mid, side, 2 * pair, at, rows, put)
        for o in range(2):
            f = 2 * pair + o
            here = (f, pl.ds(at, rows))
            copies.append(pltpu.make_async_copy(out.at[here], out_hbm.at[here], sems.at[len(copies)]))
            copies[-1].start()

    build_taps(kernel_ref, mid, side)
    for pair, chunks in ((1, ((0, 4), (4, 4))), (0, ((0, 5), (5, 3)))):
        done = 0
        for at, rows in chunks:
            for r in range(done, at + rows + 2):
                for f in range(4 if pair else 2):
                    if pair:
                        act((b_ref if f < 2 else a_ref)[f % 2, r] - mean, 2 + f, r)
                    else:
                        act(jnp.where(start, b_ref[0, r] - mean, z_ref[f, r].astype(F32) - base), f, r)
            done = at + rows + 2
            conv(pair, at, rows)
    for copy in copies:
        copy.wait()


VMEM = pl.BlockSpec(memory_space=pltpu.VMEM)
HBM = pl.BlockSpec(memory_space=pltpu.MemorySpace.HBM)
PARAMS = pltpu.CompilerParams(vmem_limit_bytes=32 * 1024 * 1024)
DMA = pltpu.SemaphoreType.DMA


def scratch(frames, rows):
    return [
        pltpu.VMEM((frames, rows, 128, 128), BF16),
        pltpu.VMEM((12 * 128, 256), BF16),
        pltpu.VMEM((9 * 128, 256), BF16),
    ]


def cost(pairs, rows):
    positions = pairs * rows * 128
    return pl.CostEstimate(
        flops=2 * positions * 36 * 128 * 256, bytes_accessed=4 << 20, transcendentals=2 * positions * 128
    )


def in_hbm(v):
    return pltpu.with_memory_space_constraint(v, pltpu.MemorySpace.HBM)


def shape(dims, dtype):
    return jax.ShapeDtypeStruct(dims, dtype)


def shards(features, gain_one, shift_one, kernel_one, bias_one, gain_two, shift_two, kernel_two, bias_two):
    slabs = lax.axis_size("tm")
    strips = lax.axis_size("space")
    devices = slabs * strips
    cells = float(4 * 8 * 128 * MEMBERS)
    swap_in = [(i, i ^ 1) for i in range(strips)]
    swap_far = [(i, (i + 1) % strips) for i in range(1, strips, 2)] + [((i + 1) % strips, i) for i in range(1, strips, 2)]
    later = [(i, (i + 1) % slabs) for i in range(slabs)]
    taps_one = kernel_one.reshape(3, 9 * 128, 128)
    taps_two = kernel_two.reshape(3, 9 * 128, 128)

    taps_one = in_hbm(taps_one)
    x, pay, z_send, in_send, far_send = pl.pallas_call(
        stats_kernel,
        out_shape=[
            shape((4, 8, 128, 128), BF16), shape((devices, 128), F32), shape((2, 8, 128, 128), BF16),
            pltpu.HBM((4, 2, 128, 128), BF16), pltpu.HBM((4, 2, 128, 128), BF16),
        ],
        in_specs=[HBM], out_specs=[VMEM] * 5,
        scratch_shapes=[DMA((4,))], compiler_params=PARAMS,
        cost_estimate=pl.CostEstimate(flops=1 << 22, bytes_accessed=1 << 20, transcendentals=0), name="stats",
    )(in_hbm(features))
    z_one = lax.ppermute(z_send, "tm", later)
    near = lax.ppermute(in_send, "space", swap_in)
    far = lax.ppermute(far_send, "space", swap_far)
    got = lax.all_to_all(pay, BOTH, 0, 0)
    near_send, far_send, taps_one, small = pl.pallas_call(
        pack_kernel, out_shape=[pltpu.HBM((2, 2, 128, 128), BF16)] * 2 + [shape((3, 9 * 128, 128), BF16), shape((6, 128), F32)],
        in_specs=[HBM] * 7 + [VMEM], out_specs=[VMEM] * 4, scratch_shapes=[DMA((7,))], compiler_params=PARAMS,
        cost_estimate=pl.CostEstimate(flops=0, bytes_accessed=1 << 19, transcendentals=0), name="pack",
    )(taps_one, *map(in_hbm, (gain_one, shift_one, bias_one, gain_two, shift_two, bias_two)), z_one)
    z_near = lax.ppermute(near_send, "space", swap_in)
    z_far = lax.ppermute(far_send, "space", swap_far)
    inner_a, send, consts = pl.pallas_call(
        functools.partial(first_kernel, False, cells, strips),
        out_shape=[shape((2, 10, 128, 128), F32), shape((2, 10, 128, 128), BF16), shape((8, 128), F32)],
        in_specs=[VMEM] * 6, out_specs=[VMEM] * 3, scratch_shapes=scratch(4, 12),
        compiler_params=PARAMS, cost_estimate=cost(1, 10), name="first_late",
    )(taps_one, got, small, x, near, far)
    z_two = lax.ppermute(send, "tm", later)
    inner_b, pay = pl.pallas_call(
        functools.partial(first_kernel, True, cells, strips),
        out_shape=[shape((2, 10, 128, 128), F32), shape((devices, 128), F32)],
        in_specs=[VMEM] * 9, out_specs=[VMEM] * 2, scratch_shapes=scratch(4, 12),
        compiler_params=PARAMS, cost_estimate=cost(1, 10), name="first_early",
    )(taps_one, consts, small, x, near, far, z_one, z_near, z_far)
    got = lax.all_to_all(pay, BOTH, 0, 0)
    return pl.pallas_call(
        functools.partial(second_kernel, cells, strips),
        out_shape=shape((4, 8, 128, 128), F32),
        in_specs=[VMEM] * 7, out_specs=HBM,
        scratch_shapes=scratch(6, 10) + [pltpu.VMEM((4, 8, 128, 128), F32), DMA((8,))],
        compiler_params=PARAMS, cost_estimate=cost(2, 8), name="second",
    )(taps_two, got, small, x, inner_b, inner_a, z_two)


def solution(mesh):
    placed = (P("tm", "space", None, None), P(), P(), P(), P(), P(), P(), P(), P())
    return jax.shard_map(
        shards, mesh=mesh, in_specs=placed, out_specs=P("tm", "space", None, None), check_vma=False
    )
```
